256 devices in a mesh: pb: 32 (over x, z_hi, core), ka: 8 (over z_lo, y).
Axes of the slice: x: 4, y: 4, z: 8 (z_hi: 4, z_lo: 2; z = z_hi * 2 + z_lo), core: 2. Of those that a mesh axis runs over, the one named last changes fastest.
Arguments:
- frame_two: bfloat16 [96, 1024, 4096], P(None, 'pb', 'ka'), may hold values from -24 to 24
- frame_band: bfloat16 [96, 9, 4096], P(None, None, 'pb'), may hold values from -24 to 24
- conv_weight: bfloat16 [9, 128, 96], replicated, may hold values from -0.21875 to 0.21875
Outputs:
- flow: float32 [2, 4, 2048], P(None, None, 'pb')
The draws below stay inside these ranges and needn't reach their ends.
All inputs are finite; a program needn't handle non-finite values.
Results may differ from the reference program's by a relative error of at most 0.0035.
The reference program's roundings to bfloat16 on the way (of `key_feats` and `query_feats`) count: a program that leaves them out, or rounds other values in their place, can miss the bound.
Values may be sent and summed in bfloat16 or wider, within the bound.
No kernel may reach another device: no remote copies, remote signals or barrier semaphores. Data moves between devices by JAX's collectives and lax.ppermute only.
A program may use at most 192 MiB of HBM per device.

```python
import math
import jax
import jax.numpy as jnp
from jax import lax

C_IN = 96
C = 128
QROWS = 4
NROWS = 512
NCOLS = 2048
BAND_TOP = 254


def clipped_normal(key, shape, spread, bound):
    return jnp.clip(spread * jax.random.normal(key, shape, jnp.float32), -bound, bound)


def draw_frame_two(key, part):
    key = jax.random.fold_in(key, 1)
    shape = (C_IN, 2 * NROWS, 2 * NCOLS)
    return clipped_normal(key, shape, 2.0, 12.0).astype(jnp.bfloat16)


def draw_frame_band(key, part):
    key = jax.random.fold_in(key, 2)
    shape = (C_IN, 2 * QROWS + 1, 2 * NCOLS)
    return clipped_normal(key, shape, 2.0, 12.0).astype(jnp.bfloat16)


def gaussian(key, shape, scale, most, kind=jnp.bfloat16):
    drawn = scale * jax.random.normal(key, shape, jnp.float32)
    return jnp.clip(drawn, min=-most, max=most).astype(kind)


def setup_inputs(seed: int = 0) -> dict:
    keys = jax.random.split(jax.random.key(seed), 4)
    return {
        "frame_two": draw_frame_two(jax.random.fold_in(keys[3], 71), 0),
        "frame_band": draw_frame_band(jax.random.fold_in(keys[3], 71), 0),
        "conv_weight": gaussian(keys[2], (9, C, C_IN), (9 * C_IN) ** -0.5, 0.21875),
    }


def conv_taps(padded, weights, out_rows, out_cols):
    total = jnp.zeros((weights.shape[1], out_rows * out_cols), jnp.float32)
    for tap_index in range(9):
        row_off = tap_index // 3
        col_off = tap_index % 3
        window = padded[:, row_off:row_off + 2 * out_rows:2, col_off:col_off + 2 * out_cols:2].astype(jnp.float32)
        window = window.reshape(window.shape[0], out_rows * out_cols)
        total = total + jnp.dot(weights[tap_index].astype(jnp.float32), window, preferred_element_type=jnp.float32)
    return total.reshape(weights.shape[1], out_rows, out_cols).astype(jnp.bfloat16)

def combine(first, second):
    highest = jnp.maximum(first[0], second[0])
    left_w = jnp.exp(first[0] - highest)
    right_w = jnp.exp(second[0] - highest)
    return (highest, first[1] * left_w + second[1] * right_w, first[2] * left_w + second[2] * right_w, first[3] * left_w + second[3] * right_w)

def block_states(queries, key_block, key_x, key_y, factor):
    scores = jnp.dot(queries.astype(jnp.float32), key_block.astype(jnp.float32), preferred_element_type=jnp.float32) * factor
    highest = lax.optimization_barrier(jnp.max(scores, axis=1))
    weights = jnp.exp(scores - highest[:, None])
    return (highest, lax.optimization_barrier(jnp.sum(weights, axis=1)), lax.optimization_barrier(jnp.sum(weights * key_x[None, :], axis=1)), lax.optimization_barrier(jnp.sum(weights * key_y[None, :], axis=1)))

def bounded_states(queries, key_feats, key_x, key_y, factor, qsize, ksize):
    n_query = queries.shape[0]
    n_key = key_feats.shape[1]
    qblk = math.gcd(n_query, qsize)
    kblk = math.gcd(n_key, ksize)
    query_blocks = queries.reshape(n_query // qblk, qblk, queries.shape[1])

    def per_query(query_block):
        start_state = (jnp.full((qblk,), -jnp.inf, jnp.float32), jnp.zeros((qblk,), jnp.float32), jnp.zeros((qblk,), jnp.float32), jnp.zeros((qblk,), jnp.float32))

        def step(running, index):
            offset = (index * kblk).astype(jnp.int32)
            feats = lax.dynamic_slice_in_dim(key_feats, offset, kblk, 1)
            block_x = lax.dynamic_slice_in_dim(key_x, offset, kblk, 0)
            block_y = lax.dynamic_slice_in_dim(key_y, offset, kblk, 0)
            return (combine(running, block_states(query_block, feats, block_x, block_y, factor)), None)
        final, unused = lax.scan(step, start_state, jnp.arange(n_key // kblk, dtype=jnp.int32))
        return final
    results = lax.map(per_query, query_blocks)
    return tuple((part.reshape(n_query) for part in results))

def reference(frame_two, frame_band, conv_weight):
    padded_two = jnp.pad(frame_two, ((0, 0), (1, 0), (1, 0)))
    key_feats = conv_taps(padded_two, conv_weight, NROWS, NCOLS).reshape(C, NROWS * NCOLS)
    padded_band = jnp.pad(frame_band, ((0, 0), (0, 0), (1, 0)))
    query_feats = conv_taps(padded_band, conv_weight, QROWS, NCOLS).reshape(C, QROWS * NCOLS).T
    row_grid = (2.0 * jnp.arange(NROWS).astype(jnp.float32) + 1.0) / NROWS - 1.0
    col_grid = (2.0 * jnp.arange(NCOLS).astype(jnp.float32) + 1.0) / NCOLS - 1.0
    key_y = jnp.repeat(row_grid, NCOLS)
    key_x = jnp.tile(col_grid, NROWS)
    factor = 1.0 / math.sqrt(C)
    states = bounded_states(query_feats, key_feats, key_x, key_y, factor, 1024, 8192)
    mean_x = (states[2] / states[1]).reshape(QROWS, NCOLS)
    mean_y = (states[3] / states[1]).reshape(QROWS, NCOLS)
    band_grid = (2.0 * (BAND_TOP + jnp.arange(QROWS)).astype(jnp.float32) + 1.0) / NROWS - 1.0
    return jnp.stack([mean_x - col_grid[None, :], mean_y - band_grid[:, None]])
```

```python
import functools
import math

import jax
import jax.numpy as jnp
from jax import lax
from jax.experimental import pallas as pl
from jax.experimental.pallas import tpu as pltpu
from jax.sharding import PartitionSpec as P

BF16 = jnp.bfloat16
F32 = jnp.float32
GROUP = 8
TAIL = 32
VMEM = 56 * 1024 * 1024


def dot(a, b):
    return jnp.dot(a, b, preferred_element_type=F32)


def dot_nt(a, b):
    return lax.dot_general(a, b, (((1,), (1,)), ((), ())), preferred_element_type=F32)


def iota(shape, axis):
    return lax.broadcasted_iota(jnp.int32, shape, axis)


def tap_selector(cols):
    half = cols // 2
    row = iota((3 * half, cols), 0)
    tap = row // half
    source = 2 * (row - tap * half) - 1 + tap
    return (iota((3 * half, cols), 1) == source).astype(BF16)


def split3(x):
    high = x.astype(BF16)
    rest = x - high.astype(F32)
    mid = rest.astype(BF16)
    low = (rest - mid.astype(F32)).astype(BF16)
    return high, mid, low


def query_kernel(band_ref, w_ref, out_ref):
    rows_in, _, cols = band_ref.shape
    rows = (rows_in - 1) // 2
    half = cols // 2
    n_query = rows * half
    channels = w_ref.shape[2]
    selector = tap_selector(cols)
    picked = [dot_nt(selector, band_ref[r]).astype(BF16) for r in range(rows_in)]
    total = jnp.zeros((n_query, channels), F32)
    beyond = jnp.zeros((rows * 16, channels), F32)
    for a in range(3):
        for b in range(3):
            lhs = jnp.concatenate(
                [picked[2 * r + a][b * half : (b + 1) * half] for r in range(rows)], axis=0
            )
            total = total + dot(lhs, w_ref[3 * a + b])
        last = jnp.concatenate(
            [picked[2 * r + a][3 * half - 16 : 3 * half] for r in range(rows)], axis=0
        )
        beyond = beyond + dot(last, w_ref[3 * a])
    out_ref[0:n_query, :] = total.astype(BF16)
    edge = jnp.concatenate(
        [total[r * half : r * half + 1] for r in range(rows)]
        + [beyond[r * 16 + 15 : r * 16 + 16] for r in range(rows)],
        axis=0,
    )
    high, mid, low = split3(edge)
    tail = jnp.concatenate(
        [high.astype(F32), mid.astype(F32), low.astype(F32), jnp.zeros_like(edge)], axis=0
    )
    out_ref[n_query:, :] = tail.astype(BF16)


def key_kernel(x_ref, w_ref, key_ref, top_ref, left_ref, below_ref, right_ref, band_ref):
    channels_in, rows_in, cols = x_ref.shape
    half = cols // 2
    channels = w_ref.shape[2]
    depth = channels_in * GROUP
    outs = GROUP // 2
    n_group = rows_in // GROUP
    expand = (iota((depth, channels_in), 0) // GROUP == iota((depth, channels_in), 1)).astype(BF16)
    row = iota((depth, channels), 0) % GROUP
    for b in range(3):
        spread = [dot(expand, w_ref[3 * a + b]) for a in range(3)]
        for i in range(outs + 1):
            block = jnp.zeros((depth, channels), F32)
            for a in range(3):
                block = jnp.where(row == 2 * i - 1 + a, spread[a], block)
            band_ref[b, :, i * channels : (i + 1) * channels] = block.astype(BF16)
    selector = tap_selector(cols)
    carried = jnp.zeros((half, channels), F32)
    carried_right = jnp.zeros((1, channels), F32)
    for g in range(n_group):
        base = (g * GROUP) // 16 * 16
        pair = x_ref[:, base : base + 16, :].astype(F32)
        off = g * GROUP - base
        x = pair[:, off : off + GROUP, :].reshape(depth, cols).astype(BF16)
        picked = dot_nt(selector, x).astype(BF16)
        total = dot(picked[0:half], band_ref[0])
        total = total + dot(picked[half : 2 * half], band_ref[1])
        total = total + dot(picked[2 * half : 3 * half], band_ref[2])
        beyond = dot(picked[3 * half - 16 : 3 * half], band_ref[0])
        for i in range(outs):
            part = total[:, i * channels : (i + 1) * channels]
            part_right = beyond[15:16, i * channels : (i + 1) * channels]
            if i == 0:
                part = part + carried
                part_right = part_right + carried_right
            o = g * outs + i
            key_ref[o * half : (o + 1) * half, :] = part.astype(BF16)
            left_ref[o] = part[0:8]
            right_ref[o : o + 1, :] = part_right
            if o == 0:
                top_ref[...] = part
        carried = total[:, outs * channels :]
        carried_right = beyond[15:16, outs * channels :]
    below_ref[0:half, :] = carried
    below_ref[half:, :] = jnp.broadcast_to(carried_right, (8, channels))


def sum_tree(parts):
    while len(parts) > 1:
        rest = [parts[-1]] if len(parts) % 2 else []
        parts = [a + b for a, b in zip(parts[0::2], parts[1::2])] + rest
    return parts[0]


def bit_tree(parts):
    if len(parts) == 1:
        return parts[0], []
    middle = len(parts) // 2
    low, low_bits = bit_tree(parts[:middle])
    high, high_bits = bit_tree(parts[middle:])
    return low + high, [a + b for a, b in zip(low_bits, high_bits)] + [high]


def attention_kernel(
    tile_rows, row_count, col_count, scale,
    place_ref, query_ref, key_ref, top_ref, left_ref, above_ref, side_ref, corner_ref, out_ref,
    keys, ext, qt,
):
    step = pl.program_id(0)
    n_block = query_ref.shape[0]
    channels = key_ref.shape[1]
    tile_cols = key_ref.shape[0] // tile_rows
    n_query = query_ref.shape[1] - TAIL
    rows = 4
    half = n_query // rows
    width = n_block * n_query

    @pl.when(step == 0)
    def _():
        ext[...] = jnp.zeros_like(ext)
        keys[...] = key_ref[...]
        top = top_ref[...] + above_ref[0:tile_cols, :]
        first = jnp.broadcast_to(side_ref[0:1, :] + corner_ref[0:1, :], top.shape)
        top = jnp.where(iota(top.shape, 0) == 0, top + first, top)
        keys[0:tile_cols, :] = top.astype(BF16)
        for i in range(1, tile_rows):
            edge = left_ref[i][0:1, :] + side_ref[i : i + 1, :]
            old = keys[i * tile_cols : i * tile_cols + 16, :].astype(F32)
            new = jnp.where(iota(old.shape, 0) == 0, jnp.broadcast_to(edge, old.shape), old)
            keys[i * tile_cols : i * tile_cols + 16, :] = new.astype(BF16)

    for p in range(n_block):
        block = query_ref[p]
        tail = block[n_query:].astype(F32)
        edge = tail[0:8] + tail[8:16] + tail[16:24]
        fixed = edge + pltpu.roll(ext[...], 4, 0)
        ext[...] = edge
        pieces = []
        for r in range(rows):
            old = block[r * half : r * half + 16].astype(F32)
            new = jnp.where(
                iota(old.shape, 0) == 0, jnp.broadcast_to(fixed[r : r + 1], old.shape), old
            )
            pieces += [new.astype(BF16), block[r * half + 16 : (r + 1) * half]]
        qt[:, p * n_query : (p + 1) * n_query] = jnp.concatenate(pieces, axis=0).T

    def scores(start, count):
        return dot(keys[pl.ds(start, count), :], qt[...])

    def write(highest, states):
        total, down, bits = states
        along = sum(float(2**b) * x for b, x in enumerate(bits))
        sub = iota(total.shape, 0).astype(F32)
        first_row = place_ref[0].astype(F32)
        first_col = place_ref[1].astype(F32)
        x = ((2.0 * (first_col + sub) + 1.0) / col_count - 1.0) * total + (16.0 / col_count) * along
        y = ((2.0 * first_row + 1.0) / row_count - 1.0) * total + (2.0 / row_count) * down
        parts = [highest] + [jnp.sum(v, axis=0, keepdims=True) for v in (total, x, y)]
        for p in range(n_block):
            lanes = slice(p * n_query, (p + 1) * n_query)
            out_ref[p] = jnp.concatenate([v[:, lanes] for v in parts], axis=0)

    def add_row(i, start, shift, states):
        total, down, bits = states
        weights = jnp.exp2(scores(start, tile_cols) * scale - shift)
        row_total, row_bits = bit_tree([weights[8 * g : 8 * g + 8] for g in range(tile_cols // 8)])
        return (
            total + row_total,
            down + i * row_total,
            tuple(a + b for a, b in zip(bits, row_bits)),
        )

    zero = jnp.zeros((8, width), F32)
    empty = (zero, zero, (zero,) * int(math.log2(tile_cols // 8)))

    sample = jnp.concatenate(
        [keys[i * tile_cols : i * tile_cols + 16, :] for i in range(tile_rows)], axis=0
    )
    highest = jnp.max(dot(sample, qt[...]), axis=0, keepdims=True) * scale
    states = empty
    for i in range(tile_rows):
        states = add_row(float(i), i * tile_cols, highest, states)
    write(highest, states)
    largest = jnp.max(states[0])

    @pl.when(jnp.logical_not(largest < 1e30))
    def _():
        def raise_max(i, top):
            start = pl.multiple_of(i * tile_cols, tile_cols)
            return jnp.maximum(top, jnp.max(scores(start, tile_cols), axis=0, keepdims=True))

        top = lax.fori_loop(0, tile_rows, raise_max, jnp.full((1, width), -jnp.inf, F32)) * scale

        def again(i, states):
            start = pl.multiple_of(i * tile_cols, tile_cols)
            return add_row(i.astype(F32), start, top, states)

        write(top, lax.fori_loop(0, tile_rows, again, empty))


def whole(shape):
    return pl.BlockSpec(shape, lambda *_: (0,) * len(shape))


def merged(states):
    highest = jnp.max(states[:, 0], axis=0)
    factor = jnp.exp2(states[:, 0] - highest[None])
    sums = jnp.sum(states[:, 1:] * factor[:, None], axis=0)
    return jnp.concatenate([highest[None], sums], axis=0)


def on_device(frame_two, frame_band, conv_weight):
    channels_in, rows_in, cols_in = frame_two.shape
    channels = conv_weight.shape[1]
    tile_rows, tile_cols = rows_in // 2, cols_in // 2
    band_rows, band_cols = (frame_band.shape[1] - 1) // 2, frame_band.shape[2] // 2
    n_pb, n_ka = lax.axis_size("pb"), lax.axis_size("ka")
    row_count, col_count = tile_rows * n_pb, tile_cols * n_ka
    pb_index, ka_index = lax.axis_index("pb"), lax.axis_index("ka")
    n_query = band_rows * band_cols
    weights = conv_weight.transpose(0, 2, 1)
    params = pltpu.CompilerParams(vmem_limit_bytes=VMEM)

    queries = pl.pallas_call(
        query_kernel,
        out_shape=jax.ShapeDtypeStruct((n_query + TAIL, channels), BF16),
        compiler_params=params,
        name="query_feats",
    )(frame_band.transpose(1, 0, 2), weights)
    queries = lax.all_gather(queries, "pb")

    n_key = tile_rows * tile_cols
    keys, top, left, below, right = pl.pallas_call(
        key_kernel,
        out_shape=(
            jax.ShapeDtypeStruct((n_key, channels), BF16),
            jax.ShapeDtypeStruct((tile_cols, channels), F32),
            jax.ShapeDtypeStruct((tile_rows, 8, channels), F32),
            jax.ShapeDtypeStruct((tile_cols + 8, channels), F32),
            jax.ShapeDtypeStruct((tile_rows, channels), F32),
        ),
        scratch_shapes=[
            pltpu.VMEM((3, channels_in * GROUP, (GROUP // 2 + 1) * channels), BF16)
        ],
        compiler_params=params,
        name="key_feats",
    )(frame_two, weights)
    above = lax.ppermute(below, "pb", [(i, i + 1) for i in range(n_pb - 1)])
    side = lax.ppermute(right, "ka", [(i, i + 1) for i in range(n_ka - 1)])
    corner = lax.ppermute(
        below[tile_cols:],
        ("pb", "ka"),
        [(p * n_ka + a, (p + 1) * n_ka + a + 1) for p in range(n_pb - 1) for a in range(n_ka - 1)],
    )

    place = jnp.stack([pb_index * tile_rows, ka_index * tile_cols]).astype(jnp.int32)
    n_block = 2
    scale = math.log2(math.e) / math.sqrt(channels)
    states = pl.pallas_call(
        functools.partial(
            attention_kernel, tile_rows, float(row_count), float(col_count), scale
        ),
        grid=(n_pb // n_block,),
        in_specs=[
            pl.BlockSpec(memory_space=pltpu.SMEM),
            pl.BlockSpec((n_block, n_query + TAIL, channels), lambda i: (i, 0, 0)),
            whole(keys.shape),
            whole(top.shape),
            whole(left.shape),
            whole(above.shape),
            whole(side.shape),
            whole(corner.shape),
        ],
        out_specs=pl.BlockSpec((n_block, 4, n_query), lambda i: (i, 0, 0)),
        out_shape=jax.ShapeDtypeStruct((n_pb, 4, n_query), F32),
        scratch_shapes=[
            pltpu.VMEM(keys.shape, BF16),
            pltpu.VMEM((8, channels), F32),
            pltpu.VMEM((channels, n_block * n_query), BF16),
        ],
        compiler_params=params,
        name="attention",
    )(place, queries, keys, top, left, above, side, corner)

    mine = merged(lax.all_to_all(states, "pb", 0, 0))
    final = merged(lax.all_to_all(jnp.broadcast_to(mine[None], (n_ka, 4, n_query)), "ka", 0, 0))
    mean_x = (final[2] / final[1]).reshape(band_rows, band_cols)
    mean_y = (final[3] / final[1]).reshape(band_rows, band_cols)
    query_x = (
        2.0 * (pb_index * band_cols + jnp.arange(band_cols, dtype=jnp.int32)).astype(F32) + 1.0
    ) / col_count - 1.0
    band_top = (row_count - band_rows) // 2
    query_y = (
        2.0 * (band_top + jnp.arange(band_rows, dtype=jnp.int32)).astype(F32) + 1.0
    ) / row_count - 1.0
    return jnp.stack([mean_x - query_x[None, :], mean_y - query_y[:, None]])


def solution(mesh):
    in_specs = (P(None, "pb", "ka"), P(None, None, "pb"), P())
    out_specs = P(None, None, "pb")
    return jax.shard_map(
        on_device, mesh=mesh, in_specs=in_specs, out_specs=out_specs, check_vma=False
    )
```

```python
import functools
import math

import jax
import jax.numpy as jnp
from jax import lax
from jax.experimental import pallas as pl
from jax.experimental.pallas import tpu as pltpu
from jax.sharding import PartitionSpec as P

BF16 = jnp.bfloat16
F32 = jnp.float32
GROUP = 8
VMEM = 56 * 1024 * 1024


def dot(a, b):
    return jnp.dot(a, b, preferred_element_type=F32)


def dot_nt(a, b):
    return lax.dot_general(a, b, (((1,), (1,)), ((), ())), preferred_element_type=F32)


def iota(shape, axis):
    return lax.broadcasted_iota(jnp.int32, shape, axis)


def tap_selector(cols):
    half = cols // 2
    row = iota((3 * half, cols), 0)
    tap = row // half
    source = 2 * (row - tap * half) - 1 + tap
    return (iota((3 * half, cols), 1) == source).astype(BF16)


def split3(x):
    high = x.astype(BF16)
    rest = x - high.astype(F32)
    mid = rest.astype(BF16)
    low = (rest - mid.astype(F32)).astype(BF16)
    return high, mid, low


def query_kernel(band_ref, w_ref, out_ref, edge_ref):
    rows_in, _, cols = band_ref.shape
    rows = (rows_in - 1) // 2
    half = cols // 2
    n_query = rows * half
    channels = w_ref.shape[2]
    selector = tap_selector(cols)
    picked = [dot_nt(selector, band_ref[r]).astype(BF16) for r in range(rows_in)]
    total = jnp.zeros((n_query, channels), F32)
    beyond = jnp.zeros((rows * 16, channels), F32)
    for a in range(3):
        for b in range(3):
            lhs = jnp.concatenate(
                [picked[2 * r + a][b * half : (b + 1) * half] for r in range(rows)], axis=0
            )
            total = total + dot(lhs, w_ref[3 * a + b])
        last = jnp.concatenate(
            [picked[2 * r + a][3 * half - 16 : 3 * half] for r in range(rows)], axis=0
        )
        beyond = beyond + dot(last, w_ref[3 * a])
    out_ref[...] = total.astype(BF16)
    edge_ref[...] = jnp.concatenate(
        [total[r * half : r * half + 1] for r in range(rows)]
        + [beyond[r * 16 + 15 : r * 16 + 16] for r in range(rows)],
        axis=0,
    )


def spread_kernel(main_ref, edge_ref, before_ref, out_ref):
    n_query = main_ref.shape[0]
    rows = edge_ref.shape[0] // 2
    half = n_query // rows
    fixed = edge_ref[0:rows, :] + before_ref[rows:, :]
    pieces = []
    for r in range(rows):
        old = main_ref[r * half : r * half + 16, :].astype(F32)
        new = jnp.where(
            iota(old.shape, 0) == 0, jnp.broadcast_to(fixed[r : r + 1], old.shape), old
        )
        pieces += [new.astype(BF16), main_ref[r * half + 16 : (r + 1) * half, :]]
    full = jnp.concatenate(pieces, axis=0)
    for i in range(out_ref.shape[0]):
        out_ref[i] = full


def key_kernel(x_ref, w_ref, key_ref, top_ref, left_ref, below_ref, right_ref, band_ref):
    channels_in, rows_in, cols = x_ref.shape
    half = cols // 2
    channels = w_ref.shape[2]
    depth = channels_in * GROUP
    outs = GROUP // 2
    n_group = rows_in // GROUP
    expand = (iota((depth, channels_in), 0) // GROUP == iota((depth, channels_in), 1)).astype(BF16)
    row = iota((depth, channels), 0) % GROUP
    for b in range(3):
        spread = [dot(expand, w_ref[3 * a + b]) for a in range(3)]
        for i in range(outs + 1):
            block = jnp.zeros((depth, channels), F32)
            for a in range(3):
                block = jnp.where(row == 2 * i - 1 + a, spread[a], block)
            band_ref[b, :, i * channels : (i + 1) * channels] = block.astype(BF16)
    selector = tap_selector(cols)
    carried = jnp.zeros((half, channels), F32)
    carried_right = jnp.zeros((1, channels), F32)
    for g in range(n_group):
        base = (g * GROUP) // 16 * 16
        pair = x_ref[:, base : base + 16, :].astype(F32)
        off = g * GROUP - base
        x = pair[:, off : off + GROUP, :].reshape(depth, cols).astype(BF16)
        picked = dot_nt(selector, x).astype(BF16)
        total = dot(picked[0:half], band_ref[0])
        total = total + dot(picked[half : 2 * half], band_ref[1])
        total = total + dot(picked[2 * half : 3 * half], band_ref[2])
        beyond = dot(picked[3 * half - 16 : 3 * half], band_ref[0])
        for i in range(outs):
            part = total[:, i * channels : (i + 1) * channels]
            part_right = beyond[15:16, i * channels : (i + 1) * channels]
            if i == 0:
                part = part + carried
                part_right = part_right + carried_right
            o = g * outs + i
            key_ref[o * half : (o + 1) * half, :] = part.astype(BF16)
            left_ref[o] = part[0:8]
            right_ref[o : o + 1, :] = part_right
            if o == 0:
                top_ref[...] = part
        carried = total[:, outs * channels :]
        carried_right = beyond[15:16, outs * channels :]
    below_ref[0:half, :] = carried
    below_ref[half:, :] = jnp.broadcast_to(carried_right, (8, channels))


def bit_tree(leaf, start, count):
    if count == 1:
        return leaf(start), []
    low, low_bits = bit_tree(leaf, start, count // 2)
    high, high_bits = bit_tree(leaf, start + count // 2, count // 2)
    return low + high, [a + b for a, b in zip(low_bits, high_bits)] + [high]


def attention_kernel(
    tile_rows, row_count, col_count, scale, second,
    place_ref, query_ref, key_ref, top_ref, left_ref, above_ref, side_ref, corner_ref, *refs,
):
    if second:
        other_ref, out_ref, keys, qt, acc = refs
    else:
        out_ref, keys, qt, acc = refs
    n_block, n_query, channels = query_ref.shape
    tile_cols = key_ref.shape[0] // tile_rows
    groups = tile_cols // 8
    n_bits = int(math.log2(groups))
    width = n_block * n_query
    chunk = min(width, 512)
    depth = keys.shape[1]

    @pl.when(pl.program_id(0) == 0)
    def _():
        pad = (keys.shape[0], depth - channels)
        keys[:, 0:channels] = key_ref[...]
        keys[:, channels:] = jnp.where(iota(pad, 1) < 3, -1.0, 0.0).astype(BF16)
        top = top_ref[...] + above_ref[0:tile_cols, :]
        first = jnp.broadcast_to(side_ref[0:1, :] + corner_ref[0:1, :], top.shape)
        top = jnp.where(iota(top.shape, 0) == 0, top + first, top)
        keys[0:tile_cols, 0:channels] = top.astype(BF16)
        for i in range(1, tile_rows):
            edge = left_ref[i][0:1, :] + side_ref[i : i + 1, :]
            rows = slice(i * tile_cols, i * tile_cols + 16)
            old = keys[rows, 0:channels].astype(F32)
            new = jnp.where(iota(old.shape, 0) == 0, jnp.broadcast_to(edge, old.shape), old)
            keys[rows, 0:channels] = new.astype(BF16)

    def set_shift(shift):
        parts = split3(shift) + (jnp.zeros((depth - channels - 3, width), BF16),)
        qt[channels:, :] = jnp.concatenate([v.astype(F32) for v in parts], axis=0).astype(BF16)

    for p in range(n_block):
        qt[0:channels, p * n_query : (p + 1) * n_query] = query_ref[p].T

    def add_row(i, start):
        for h in range(width // chunk):
            scores = dot(keys[pl.ds(start, tile_cols), :], qt[:, h * chunk : (h + 1) * chunk])
            for l in range(chunk // 128):
                lanes = slice(h * chunk + l * 128, h * chunk + (l + 1) * 128)

                def leaf(g):
                    return jnp.exp2(scores[8 * g : 8 * g + 8, l * 128 : (l + 1) * 128] * scale)

                total, bits = bit_tree(leaf, 0, groups)
                for n, v in enumerate([total, i * total] + bits):
                    acc[n, :, lanes] += v

    def write(shift):
        total, down = acc[0], acc[1]
        along = sum(float(2**b) * acc[2 + b] for b in range(n_bits))
        sub = iota(total.shape, 0).astype(F32)
        first_row = place_ref[0].astype(F32)
        first_col = place_ref[1].astype(F32)
        x = ((2.0 * (first_col + sub) + 1.0) / col_count - 1.0) * total + (16.0 / col_count) * along
        y = ((2.0 * first_row + 1.0) / row_count - 1.0) * total + (2.0 / row_count) * down
        parts = [shift] + [jnp.sum(v, axis=0, keepdims=True) for v in (total, x, y)]
        for p in range(n_block):
            lanes = slice(p * n_query, (p + 1) * n_query)
            block = jnp.concatenate([v[:, lanes] for v in parts], axis=0)
            if second:
                out_ref[p, 1 - place_ref[2]] = block
                out_ref[p, place_ref[2]] = other_ref[p]
            else:
                out_ref[p] = block

    sample = jnp.concatenate(
        [keys[i * tile_cols : i * tile_cols + 16, 0:channels] for i in range(tile_rows)], axis=0
    )
    shift = jnp.max(dot(sample, qt[0:channels, :]), axis=0, keepdims=True)
    set_shift(shift)
    acc[...] = jnp.zeros_like(acc)
    for i in range(tile_rows):
        add_row(float(i), i * tile_cols)
    write(shift)

    @pl.when(jnp.logical_not(jnp.max(acc[0]) < 1e30))
    def _():
        def raise_max(i, top):
            start = pl.multiple_of(i * tile_cols, tile_cols)
            scores = dot(keys[pl.ds(start, tile_cols), 0:channels], qt[0:channels, :])
            return jnp.maximum(top, jnp.max(scores, axis=0, keepdims=True))

        top = lax.fori_loop(0, tile_rows, raise_max, jnp.full((1, width), -jnp.inf, F32))
        set_shift(top)
        acc[...] = jnp.zeros_like(acc)

        def again(i, carry):
            add_row(i.astype(F32), pl.multiple_of(i * tile_cols, tile_cols))
            return carry

        lax.fori_loop(0, tile_rows, again, 0)
        write(top)


def whole(shape):
    return pl.BlockSpec(shape, lambda *_: (0,) * len(shape))


def merged(states, scale):
    highest = jnp.max(states[:, 0], axis=0)
    factor = jnp.exp2((states[:, 0] - highest[None]) * scale)
    sums = jnp.sum(states[:, 1:] * factor[:, None], axis=0)
    return jnp.concatenate([highest[None], sums], axis=0)


def on_device(frame_two, frame_band, conv_weight):
    channels_in, rows_in, cols_in = frame_two.shape
    channels = conv_weight.shape[1]
    tile_rows, tile_cols = rows_in // 2, cols_in // 2
    band_rows, band_cols = (frame_band.shape[1] - 1) // 2, frame_band.shape[2] // 2
    pb = ("chip", "core")
    n_chip, n_pb, n_ka = lax.axis_size("chip"), lax.axis_size(pb), lax.axis_size("ka")
    row_count, col_count = tile_rows * n_pb, tile_cols * n_ka
    pb_index, ka_index = lax.axis_index(pb), lax.axis_index("ka")
    n_query = band_rows * band_cols
    weights = conv_weight.transpose(0, 2, 1)
    params = pltpu.CompilerParams(vmem_limit_bytes=VMEM)

    main, edge = pl.pallas_call(
        query_kernel,
        out_shape=(
            jax.ShapeDtypeStruct((n_query, channels), BF16),
            jax.ShapeDtypeStruct((2 * band_rows, channels), F32),
        ),
        compiler_params=params,
        name="query_feats",
    )(frame_band.transpose(1, 0, 2), weights)
    before = lax.ppermute(edge, pb, [(i, i + 1) for i in range(n_pb - 1)])
    copies = pl.pallas_call(
        spread_kernel,
        out_shape=jax.ShapeDtypeStruct((n_chip, n_query, channels), BF16),
        compiler_params=params,
        name="query_copies",
    )(main, edge, before)
    queries = lax.all_to_all(copies, "chip", 0, 0)

    n_key = tile_rows * tile_cols
    keys, top, left, below, right = pl.pallas_call(
        key_kernel,
        out_shape=(
            jax.ShapeDtypeStruct((n_key, channels), BF16),
            jax.ShapeDtypeStruct((tile_cols, channels), F32),
            jax.ShapeDtypeStruct((tile_rows, 8, channels), F32),
            jax.ShapeDtypeStruct((tile_cols + 8, channels), F32),
            jax.ShapeDtypeStruct((tile_rows, channels), F32),
        ),
        scratch_shapes=[
            pltpu.VMEM((3, channels_in * GROUP, (GROUP // 2 + 1) * channels), BF16)
        ],
        compiler_params=params,
        name="key_feats",
    )(frame_two, weights)
    above = lax.ppermute(below, pb, [(i, i + 1) for i in range(n_pb - 1)])
    side = lax.ppermute(right, "ka", [(i, i + 1) for i in range(n_ka - 1)])
    corner = lax.ppermute(
        below[tile_cols:],
        ("chip", "core", "ka"),
        [(p * n_ka + a, (p + 1) * n_ka + a + 1) for p in range(n_pb - 1) for a in range(n_ka - 1)],
    )
    queries, above, side, corner = lax.optimization_barrier((queries, above, side, corner))
    twins = lax.ppermute(queries, "core", [(0, 1), (1, 0)])

    place = jnp.stack(
        [pb_index * tile_rows, ka_index * tile_cols, lax.axis_index("core")]
    ).astype(jnp.int32)
    n_block = 4
    scale = math.log2(math.e) / math.sqrt(channels)

    def attend(block, other):
        ins = [keys, top, left, above, side, corner]
        in_specs = [
            pl.BlockSpec(memory_space=pltpu.SMEM),
            pl.BlockSpec((n_block, n_query, channels), lambda i: (i, 0, 0)),
        ] + [whole(v.shape) for v in ins]
        if other is None:
            out_spec = pl.BlockSpec((n_block, 4, n_query), lambda i: (i, 0, 0))
            out_shape = (n_chip, 4, n_query)
        else:
            ins.append(other)
            in_specs.append(pl.BlockSpec((n_block, 4, n_query), lambda i: (i, 0, 0)))
            out_spec = pl.BlockSpec((n_block, 2, 4, n_query), lambda i: (i, 0, 0, 0))
            out_shape = (n_chip, 2, 4, n_query)
        return pl.pallas_call(
            functools.partial(
                attention_kernel,
                tile_rows, float(row_count), float(col_count), scale, other is not None,
            ),
            grid=(n_chip // n_block,),
            in_specs=in_specs,
            out_specs=out_spec,
            out_shape=jax.ShapeDtypeStruct(out_shape, F32),
            scratch_shapes=[
                pltpu.VMEM((n_key, channels + 16), BF16),
                pltpu.VMEM((channels + 16, n_block * n_query), BF16),
                pltpu.VMEM((2 + int(math.log2(tile_cols // 8)), 8, n_block * n_query), F32),
            ],
            compiler_params=params,
            name="attention",
        )(place, block, *ins)

    states = attend(twins, attend(queries, None)).reshape(n_pb, 4, n_query)
    mine = merged(lax.all_to_all(states, pb, 0, 0), scale)
    copies = jnp.broadcast_to(mine[None], (n_ka, 4, n_query))
    final = merged(lax.all_to_all(copies, "ka", 0, 0), scale)
    mean_x = (final[2] / final[1]).reshape(band_rows, band_cols)
    mean_y = (final[3] / final[1]).reshape(band_rows, band_cols)
    query_x = (
        2.0 * (pb_index * band_cols + jnp.arange(band_cols, dtype=jnp.int32)).astype(F32) + 1.0
    ) / col_count - 1.0
    band_top = (row_count - band_rows) // 2
    query_y = (
        2.0 * (band_top + jnp.arange(band_rows, dtype=jnp.int32)).astype(F32) + 1.0
    ) / row_count - 1.0
    return jnp.stack([mean_x - query_x[None, :], mean_y - query_y[:, None]])


def solution(mesh):
    n_pb, n_ka = mesh.shape["pb"], mesh.shape["ka"]
    finer = jax.sharding.Mesh(
        mesh.devices.reshape(n_pb // 2, 2, n_ka), ("chip", "core", "ka")
    )
    pb = ("chip", "core")
    in_specs = (P(None, pb, "ka"), P(None, None, pb), P())
    out_specs = P(None, None, pb)
    return jax.shard_map(
        on_device, mesh=finer, in_specs=in_specs, out_specs=out_specs, check_vma=False
    )
```

```python
import functools
import math

import jax
import jax.numpy as jnp
from jax import lax
from jax.experimental import pallas as pl
from jax.experimental.pallas import tpu as pltpu
from jax.sharding import PartitionSpec as P

BF16 = jnp.bfloat16
F32 = jnp.float32
GROUP = 8
VMEM = 56 * 1024 * 1024


def dot(a, b):
    return jnp.dot(a, b, preferred_element_type=F32)


def dot_nt(a, b):
    return lax.dot_general(a, b, (((1,), (1,)), ((), ())), preferred_element_type=F32)


def iota(shape, axis):
    return lax.broadcasted_iota(jnp.int32, shape, axis)


def tap_selector(cols):
    half = cols // 2
    row = iota((3 * half, cols), 0)
    tap = row // half
    source = 2 * (row - tap * half) - 1 + tap
    return (iota((3 * half, cols), 1) == source).astype(BF16)


def split3(x):
    high = x.astype(BF16)
    rest = x - high.astype(F32)
    mid = rest.astype(BF16)
    low = (rest - mid.astype(F32)).astype(BF16)
    return high, mid, low


def last_lane(x):
    rows, cols = x.shape
    picker = (iota((16, cols), 1) == cols - 1).astype(BF16)
    return dot_nt(picker, x)


def group_of(x_ref, g):
    channels_in, _, cols = x_ref.shape
    base = (g * GROUP) // 16 * 16
    pair = x_ref[:, base : base + 16, :].astype(F32)
    off = g * GROUP - base
    return pair[:, off : off + GROUP, :].reshape(channels_in * GROUP, cols).astype(BF16)


def query_kernel(band_ref, w_ref, bottom_ref, right_ref, out_ref, edge_ref, down_ref, side_ref):
    rows_in, channels_in, cols = band_ref.shape
    rows = (rows_in - 1) // 2
    half = cols // 2
    n_query = rows * half
    channels = w_ref.shape[2]
    selector = tap_selector(cols)
    picked = [dot_nt(selector, band_ref[r]).astype(BF16) for r in range(rows_in)]
    total = jnp.zeros((n_query, channels), F32)
    beyond = jnp.zeros((rows * 16, channels), F32)
    for a in range(3):
        for b in range(3):
            lhs = jnp.concatenate(
                [picked[2 * r + a][b * half : (b + 1) * half] for r in range(rows)], axis=0
            )
            total = total + dot(lhs, w_ref[3 * a + b])
        last = jnp.concatenate(
            [picked[2 * r + a][3 * half - 16 : 3 * half] for r in range(rows)], axis=0
        )
        beyond = beyond + dot(last, w_ref[3 * a])
    out_ref[...] = total.astype(BF16)
    edge_ref[...] = jnp.concatenate(
        [total[r * half : r * half + 1] for r in range(rows)] * 2, axis=0
    )

    depth = channels_in * GROUP
    wide = bottom_ref.shape[2]
    picker = (iota((channels_in, depth), 1) == iota((channels_in, depth), 0) * GROUP + GROUP - 1)
    last_group = bottom_ref.shape[1] // GROUP - 1
    bottom = dot(picker.astype(BF16), group_of(bottom_ref, last_group))
    down_ref[0:channels_in, :] = bottom.astype(BF16)
    ext = jnp.concatenate(
        [beyond[r * 16 + 15 : r * 16 + 16] for r in range(rows)]
        + [jnp.zeros((16 - rows, channels), F32)],
        axis=0,
    )
    parts = [v.astype(F32) for v in split3(ext)]
    blank = jnp.zeros((16, wide - 3 * channels), F32)
    down_ref[channels_in:, :] = jnp.concatenate(parts + [blank], axis=1).astype(BF16)

    side = jnp.zeros((16, depth), F32)
    for g in range(right_ref.shape[1] // GROUP):
        side = jnp.where(iota(side.shape, 0) == g, last_lane(group_of(right_ref, g)), side)
    side_ref[...] = side.astype(BF16)


def spread_kernel(main_ref, edge_ref, down_ref, side_ref, out_ref, corner_ref):
    n_query, channels = main_ref.shape
    rows = edge_ref.shape[0] // 2
    half = n_query // rows
    depth = side_ref.shape[1]
    channels_in = depth // GROUP
    wide = down_ref.shape[1]
    tail = down_ref[channels_in:, :].astype(F32)
    before = sum(tail[:, n * channels : (n + 1) * channels] for n in range(3))
    fixed = edge_ref[...] + before[0:8]
    pieces = []
    for r in range(rows):
        old = main_ref[r * half : r * half + 16, :].astype(F32)
        new = jnp.where(
            iota(old.shape, 0) == 0, jnp.broadcast_to(fixed[r : r + 1], old.shape), old
        )
        pieces += [new.astype(BF16), main_ref[r * half + 16 : (r + 1) * half, :]]
    full = jnp.concatenate(pieces, axis=0)
    for i in range(out_ref.shape[0]):
        out_ref[i] = full
    row = down_ref[0:channels_in, wide - 128 :]
    row = jnp.concatenate([row, jnp.zeros((depth - channels_in, 128), BF16)], axis=0)
    side = side_ref[...].astype(F32)
    corner_ref[...] = jnp.where(iota(side.shape, 0) == 8, last_lane(row), side).astype(BF16)


def key_kernel(x_ref, w_ref, above_ref, side_ref, key_ref, band_ref):
    channels_in, rows_in, cols = x_ref.shape
    half = cols // 2
    channels = w_ref.shape[2]
    depth = channels_in * GROUP
    outs = GROUP // 2
    n_group = rows_in // GROUP
    expand = (iota((depth, channels_in), 0) // GROUP == iota((depth, channels_in), 1)).astype(BF16)
    row = iota((depth, channels), 0) % GROUP
    for b in range(3):
        spread = [dot(expand, w_ref[3 * a + b]) for a in range(3)]
        for i in range(outs + 1):
            block = jnp.zeros((depth, channels), F32)
            for a in range(3):
                block = jnp.where(row == 2 * i - 1 + a, spread[a], block)
            band_ref[b, :, i * channels : (i + 1) * channels] = block.astype(BF16)
    selector = tap_selector(cols)
    side = side_ref[...].astype(F32)

    def taps(x, left):
        picked = dot_nt(selector, x)
        first = picked[0:half]
        first = jnp.where(iota(first.shape, 0) == 0, jnp.broadcast_to(left, first.shape), first)
        return first.astype(BF16), picked[half : 2 * half].astype(BF16), picked[2 * half :].astype(BF16)

    upper = taps(above_ref[0:channels_in, :], side[8:9, 0:channels_in])
    carried = sum(dot(upper[b], w_ref[b]) for b in range(3))
    for g in range(n_group):
        picked = taps(group_of(x_ref, g), side[g : g + 1])
        total = sum(dot(picked[b], band_ref[b]) for b in range(3))
        for i in range(outs):
            part = total[:, i * channels : (i + 1) * channels]
            if i == 0:
                part = part + carried
            o = g * outs + i
            key_ref[o * half : (o + 1) * half, 0:channels] = part.astype(BF16)
        carried = total[:, outs * channels :]
    pad = (key_ref.shape[0], key_ref.shape[1] - channels)
    key_ref[:, channels:] = jnp.where(iota(pad, 1) < 3, -1.0, 0.0).astype(BF16)


def bit_tree(leaf, start, count):
    if count == 1:
        return leaf(start), []
    low, low_bits = bit_tree(leaf, start, count // 2)
    high, high_bits = bit_tree(leaf, start + count // 2, count // 2)
    return low + high, [a + b for a, b in zip(low_bits, high_bits)] + [high]


def attention_kernel(
    tile_rows, row_count, col_count, scale, second,
    place_ref, query_ref, keys, *refs,
):
    if second:
        other_ref, out_ref, qt, acc = refs
    else:
        out_ref, qt, acc = refs
    n_block, n_query, channels = query_ref.shape
    tile_cols = keys.shape[0] // tile_rows
    groups = tile_cols // 8
    n_bits = int(math.log2(groups))
    width = n_block * n_query
    chunk = min(width, 512)
    depth = keys.shape[1]

    def set_shift(shift):
        parts = split3(shift) + (jnp.zeros((depth - channels - 3, width), BF16),)
        qt[channels:, :] = jnp.concatenate([v.astype(F32) for v in parts], axis=0).astype(BF16)

    for p in range(n_block):
        qt[0:channels, p * n_query : (p + 1) * n_query] = query_ref[p].T

    def add_row(i, start):
        for h in range(width // chunk):
            scores = dot(keys[pl.ds(start, tile_cols), :], qt[:, h * chunk : (h + 1) * chunk])
            for l in range(chunk // 128):
                lanes = slice(h * chunk + l * 128, h * chunk + (l + 1) * 128)

                def leaf(g):
                    return jnp.exp2(scores[8 * g : 8 * g + 8, l * 128 : (l + 1) * 128] * scale)

                total, bits = bit_tree(leaf, 0, groups)
                for n, v in enumerate([total, i * total] + bits):
                    acc[n, :, lanes] += v

    def write(shift):
        total, down = acc[0], acc[1]
        along = sum(float(2**b) * acc[2 + b] for b in range(n_bits))
        sub = iota(total.shape, 0).astype(F32)
        first_row = place_ref[0].astype(F32)
        first_col = place_ref[1].astype(F32)
        x = ((2.0 * (first_col + sub) + 1.0) / col_count - 1.0) * total + (16.0 / col_count) * along
        y = ((2.0 * first_row + 1.0) / row_count - 1.0) * total + (2.0 / row_count) * down
        parts = [shift] + [jnp.sum(v, axis=0, keepdims=True) for v in (total, x, y)]
        for p in range(n_block):
            lanes = slice(p * n_query, (p + 1) * n_query)
            block = jnp.concatenate([v[:, lanes] for v in parts], axis=0)
            if second:
                out_ref[p, 1 - place_ref[2]] = block
                out_ref[p, place_ref[2]] = other_ref[p]
            else:
                out_ref[p] = block

    sample = jnp.concatenate(
        [keys[i * tile_cols : i * tile_cols + 16, 0:channels] for i in range(tile_rows)], axis=0
    )
    shift = jnp.max(dot(sample, qt[0:channels, :]), axis=0, keepdims=True)
    set_shift(shift)
    acc[...] = jnp.zeros_like(acc)
    for i in range(tile_rows):
        add_row(float(i), i * tile_cols)
    write(shift)

    @pl.when(jnp.logical_not(jnp.max(acc[0]) < 1e30))
    def _():
        def raise_max(i, top):
            start = pl.multiple_of(i * tile_cols, tile_cols)
            scores = dot(keys[pl.ds(start, tile_cols), 0:channels], qt[0:channels, :])
            return jnp.maximum(top, jnp.max(scores, axis=0, keepdims=True))

        top = lax.fori_loop(0, tile_rows, raise_max, jnp.full((1, width), -jnp.inf, F32))
        set_shift(top)
        acc[...] = jnp.zeros_like(acc)

        def again(i, carry):
            add_row(i.astype(F32), pl.multiple_of(i * tile_cols, tile_cols))
            return carry

        lax.fori_loop(0, tile_rows, again, 0)
        write(top)


def whole(shape):
    return pl.BlockSpec(shape, lambda *_: (0,) * len(shape))


def merged(states, scale):
    highest = jnp.max(states[:, 0], axis=0)
    factor = jnp.exp2((states[:, 0] - highest[None]) * scale)
    sums = jnp.sum(states[:, 1:] * factor[:, None], axis=0)
    return jnp.concatenate([highest[None], sums], axis=0)


def on_device(frame_two, frame_band, conv_weight):
    channels_in, rows_in, cols_in = frame_two.shape
    channels = conv_weight.shape[1]
    tile_rows, tile_cols = rows_in // 2, cols_in // 2
    band_rows, band_cols = (frame_band.shape[1] - 1) // 2, frame_band.shape[2] // 2
    pb = ("chip", "core")
    n_chip, n_pb, n_ka = lax.axis_size("chip"), lax.axis_size(pb), lax.axis_size("ka")
    row_count, col_count = tile_rows * n_pb, tile_cols * n_ka
    pb_index, ka_index = lax.axis_index(pb), lax.axis_index("ka")
    n_query = band_rows * band_cols
    weights = conv_weight.transpose(0, 2, 1)
    params = pltpu.CompilerParams(vmem_limit_bytes=VMEM)

    depth = channels_in * GROUP
    whole_band = (band_rows * 2 + 1, channels_in, 2 * band_cols)
    outs = (
        jax.ShapeDtypeStruct((n_query, channels), BF16),
        jax.ShapeDtypeStruct((2 * band_rows, channels), F32),
        jax.ShapeDtypeStruct((channels_in + 16, cols_in), BF16),
        jax.ShapeDtypeStruct((16, depth), BF16),
    )
    main, edge, down, right = pl.pallas_call(
        query_kernel,
        grid=(1,),
        in_specs=[
            whole(whole_band),
            whole(weights.shape),
            pl.BlockSpec((channels_in, 16, cols_in), lambda i: (0, rows_in // 16 - 1, 0)),
            pl.BlockSpec((channels_in, rows_in, 128), lambda i: (0, 0, cols_in // 128 - 1)),
        ],
        out_specs=[whole(v.shape) for v in outs],
        out_shape=outs,
        compiler_params=params,
        name="query_feats",
    )(frame_band.transpose(1, 0, 2), weights, frame_two, frame_two)
    above = lax.ppermute(down, pb, [(i, i + 1) for i in range(n_pb - 1)])
    copies, right = pl.pallas_call(
        spread_kernel,
        out_shape=(jax.ShapeDtypeStruct((n_chip, n_query, channels), BF16), outs[3]),
        compiler_params=params,
        name="query_copies",
    )(main, edge, above, right)
    side = lax.ppermute(right, "ka", [(i, i + 1) for i in range(n_ka - 1)])
    queries = lax.all_to_all(copies, "chip", 0, 0)

    n_key = tile_rows * tile_cols
    keys = pl.pallas_call(
        key_kernel,
        out_shape=jax.ShapeDtypeStruct((n_key, channels + 16), BF16),
        scratch_shapes=[pltpu.VMEM((3, depth, (GROUP // 2 + 1) * channels), BF16)],
        compiler_params=params,
        name="key_feats",
    )(frame_two, weights, above, side)
    queries, keys = lax.optimization_barrier((queries, keys))
    twins = lax.ppermute(queries, "core", [(0, 1), (1, 0)])

    place = jnp.stack(
        [pb_index * tile_rows, ka_index * tile_cols, lax.axis_index("core")]
    ).astype(jnp.int32)
    n_block = 4
    scale = math.log2(math.e) / math.sqrt(channels)

    def attend(block, other):
        ins = [keys]
        in_specs = [
            pl.BlockSpec(memory_space=pltpu.SMEM),
            pl.BlockSpec((n_block, n_query, channels), lambda i: (i, 0, 0)),
        ] + [whole(v.shape) for v in ins]
        if other is None:
            out_spec = pl.BlockSpec((n_block, 4, n_query), lambda i: (i, 0, 0))
            out_shape = (n_chip, 4, n_query)
        else:
            ins.append(other)
            in_specs.append(pl.BlockSpec((n_block, 4, n_query), lambda i: (i, 0, 0)))
            out_spec = pl.BlockSpec((n_block, 2, 4, n_query), lambda i: (i, 0, 0, 0))
            out_shape = (n_chip, 2, 4, n_query)
        return pl.pallas_call(
            functools.partial(
                attention_kernel,
                tile_rows, float(row_count), float(col_count), scale, other is not None,
            ),
            grid=(n_chip // n_block,),
            in_specs=in_specs,
            out_specs=out_spec,
            out_shape=jax.ShapeDtypeStruct(out_shape, F32),
            scratch_shapes=[
                pltpu.VMEM((channels + 16, n_block * n_query), BF16),
                pltpu.VMEM((2 + int(math.log2(tile_cols // 8)), 8, n_block * n_query), F32),
            ],
            compiler_params=params,
            name="attention",
        )(place, block, *ins)

    states = attend(twins, attend(queries, None)).reshape(n_pb, 4, n_query)
    mine = merged(lax.all_to_all(states, pb, 0, 0), scale)
    copies = jnp.broadcast_to(mine[None], (n_ka, 4, n_query))
    final = merged(lax.all_to_all(copies, "ka", 0, 0), scale)
    mean_x = (final[2] / final[1]).reshape(band_rows, band_cols)
    mean_y = (final[3] / final[1]).reshape(band_rows, band_cols)
    query_x = (
        2.0 * (pb_index * band_cols + jnp.arange(band_cols, dtype=jnp.int32)).astype(F32) + 1.0
    ) / col_count - 1.0
    band_top = (row_count - band_rows) // 2
    query_y = (
        2.0 * (band_top + jnp.arange(band_rows, dtype=jnp.int32)).astype(F32) + 1.0
    ) / row_count - 1.0
    return jnp.stack([mean_x - query_x[None, :], mean_y - query_y[:, None]])


def solution(mesh):
    n_pb, n_ka = mesh.shape["pb"], mesh.shape["ka"]
    finer = jax.sharding.Mesh(
        mesh.devices.reshape(n_pb // 2, 2, n_ka), ("chip", "core", "ka")
    )
    pb = ("chip", "core")
    in_specs = (P(None, pb, "ka"), P(None, None, pb), P())
    out_specs = P(None, None, pb)
    return jax.shard_map(
        on_device, mesh=finer, in_specs=in_specs, out_specs=out_specs, check_vma=False
    )
```

```python
import functools
import math

import jax
import jax.numpy as jnp
from jax import lax
from jax.experimental import pallas as pl
from jax.experimental.pallas import tpu as pltpu
from jax.sharding import PartitionSpec as P

BF16 = jnp.bfloat16
F32 = jnp.float32
GROUP = 8
VMEM = 56 * 1024 * 1024


def dot(a, b):
    return jnp.dot(a, b, preferred_element_type=F32)


def dot_nt(a, b):
    return lax.dot_general(a, b, (((1,), (1,)), ((), ())), preferred_element_type=F32)


def iota(shape, axis):
    return lax.broadcasted_iota(jnp.int32, shape, axis)


def tap_selector(cols):
    half = cols // 2
    row = iota((3 * half, cols), 0)
    tap = row // half
    source = 2 * (row - tap * half) - 1 + tap
    return (iota((3 * half, cols), 1) == source).astype(BF16)


def split3(x):
    high = x.astype(BF16)
    rest = x - high.astype(F32)
    mid = rest.astype(BF16)
    low = (rest - mid.astype(F32)).astype(BF16)
    return high, mid, low


def last_lane(x):
    rows, cols = x.shape
    picker = (iota((16, cols), 1) == cols - 1).astype(BF16)
    return dot_nt(picker, x)


def group_of(x_ref, g):
    channels_in, _, cols = x_ref.shape
    base = (g * GROUP) // 16 * 16
    pair = x_ref[:, base : base + 16, :].astype(F32)
    off = g * GROUP - base
    return pair[:, off : off + GROUP, :].reshape(channels_in * GROUP, cols).astype(BF16)


def query_kernel(band_ref, w_ref, bottom_ref, right_ref, out_ref, edge_ref, down_ref, side_ref):
    rows_in, channels_in, cols = band_ref.shape
    rows = (rows_in - 1) // 2
    half = cols // 2
    n_query = rows * half
    channels = w_ref.shape[2]
    selector = tap_selector(cols)
    picked = [dot_nt(selector, band_ref[r]).astype(BF16) for r in range(rows_in)]
    total = jnp.zeros((n_query, channels), F32)
    beyond = jnp.zeros((rows * 16, channels), F32)
    for a in range(3):
        for b in range(3):
            lhs = jnp.concatenate(
                [picked[2 * r + a][b * half : (b + 1) * half] for r in range(rows)], axis=0
            )
            total = total + dot(lhs, w_ref[3 * a + b])
        last = jnp.concatenate(
            [picked[2 * r + a][3 * half - 16 : 3 * half] for r in range(rows)], axis=0
        )
        beyond = beyond + dot(last, w_ref[3 * a])
    out_ref[...] = total.astype(BF16)
    edge_ref[...] = jnp.concatenate(
        [total[r * half : r * half + 1] for r in range(rows)] * 2, axis=0
    )

    depth = channels_in * GROUP
    wide = bottom_ref.shape[2]
    picker = (iota((channels_in, depth), 1) == iota((channels_in, depth), 0) * GROUP + GROUP - 1)
    last_group = bottom_ref.shape[1] // GROUP - 1
    bottom = dot(picker.astype(BF16), group_of(bottom_ref, last_group))
    down_ref[0:channels_in, :] = bottom.astype(BF16)
    ext = jnp.concatenate(
        [beyond[r * 16 + 15 : r * 16 + 16] for r in range(rows)]
        + [jnp.zeros((16 - rows, channels), F32)],
        axis=0,
    )
    parts = [v.astype(F32) for v in split3(ext)]
    blank = jnp.zeros((16, wide - 3 * channels), F32)
    down_ref[channels_in:, :] = jnp.concatenate(parts + [blank], axis=1).astype(BF16)

    side = jnp.zeros((16, depth), F32)
    for g in range(right_ref.shape[1] // GROUP):
        side = jnp.where(iota(side.shape, 0) == g, last_lane(group_of(right_ref, g)), side)
    side_ref[...] = side.astype(BF16)


def spread_kernel(main_ref, edge_ref, down_ref, side_ref, out_ref, corner_ref):
    n_query, channels = main_ref.shape
    rows = edge_ref.shape[0] // 2
    half = n_query // rows
    depth = side_ref.shape[1]
    channels_in = depth // GROUP
    wide = down_ref.shape[1]
    tail = down_ref[channels_in:, :].astype(F32)
    before = sum(tail[:, n * channels : (n + 1) * channels] for n in range(3))
    fixed = edge_ref[...] + before[0:8]
    pieces = []
    for r in range(rows):
        old = main_ref[r * half : r * half + 16, :].astype(F32)
        new = jnp.where(
            iota(old.shape, 0) == 0, jnp.broadcast_to(fixed[r : r + 1], old.shape), old
        )
        pieces += [new.astype(BF16), main_ref[r * half + 16 : (r + 1) * half, :]]
    full = jnp.concatenate(pieces, axis=0)
    for i in range(out_ref.shape[0]):
        out_ref[i] = full
    row = down_ref[0:channels_in, wide - 128 :]
    row = jnp.concatenate([row, jnp.zeros((depth - channels_in, 128), BF16)], axis=0)
    side = side_ref[...].astype(F32)
    corner_ref[...] = jnp.where(iota(side.shape, 0) == 8, last_lane(row), side).astype(BF16)


def key_kernel(x_ref, w_ref, above_ref, side_ref, key_ref, band_ref):
    channels_in, rows_in, cols = x_ref.shape
    half = cols // 2
    channels = w_ref.shape[2]
    depth = channels_in * GROUP
    outs = GROUP // 2
    n_group = rows_in // GROUP
    expand = (iota((depth, channels_in), 0) // GROUP == iota((depth, channels_in), 1)).astype(BF16)
    row = iota((depth, channels), 0) % GROUP
    for b in range(3):
        spread = [dot(expand, w_ref[3 * a + b]) for a in range(3)]
        for i in range(outs + 1):
            block = jnp.zeros((depth, channels), F32)
            for a in range(3):
                block = jnp.where(row == 2 * i - 1 + a, spread[a], block)
            band_ref[b, :, i * channels : (i + 1) * channels] = block.astype(BF16)
    selector = tap_selector(cols)
    side = side_ref[...].astype(F32)

    def taps(x, left):
        picked = dot_nt(selector, x)
        first = picked[0:half]
        first = jnp.where(iota(first.shape, 0) == 0, jnp.broadcast_to(left, first.shape), first)
        return first.astype(BF16), picked[half : 2 * half].astype(BF16), picked[2 * half :].astype(BF16)

    upper = taps(above_ref[0:channels_in, :], side[8:9, 0:channels_in])
    carried = sum(dot(upper[b], w_ref[b]) for b in range(3))
    for g in range(n_group):
        picked = taps(group_of(x_ref, g), side[g : g + 1])
        total = sum(dot(picked[b], band_ref[b]) for b in range(3))
        for i in range(outs):
            part = total[:, i * channels : (i + 1) * channels]
            if i == 0:
                part = part + carried
            o = g * outs + i
            key_ref[o * half : (o + 1) * half, 0:channels] = part.astype(BF16)
        carried = total[:, outs * channels :]
    pad = (key_ref.shape[0], key_ref.shape[1] - channels)
    key_ref[:, channels:] = jnp.where(iota(pad, 1) < 3, -1.0, 0.0).astype(BF16)


def bit_tree(leaf, start, count):
    if count == 1:
        return leaf(start), []
    low, low_bits = bit_tree(leaf, start, count // 2)
    high, high_bits = bit_tree(leaf, start + count // 2, count // 2)
    return low + high, [a + b for a, b in zip(low_bits, high_bits)] + [high]


def attention_kernel(
    tile_rows, row_count, col_count, scale, second,
    place_ref, query_ref, keys, *refs,
):
    if second:
        other_ref, out_ref, qt, acc = refs
    else:
        out_ref, qt, acc = refs
    n_block, n_query, channels = query_ref.shape
    tile_cols = keys.shape[0] // tile_rows
    groups = tile_cols // 8
    n_bits = int(math.log2(groups))
    width = n_block * n_query
    chunk = min(width, 512)
    depth = keys.shape[1]

    def set_shift(shift):
        parts = split3(shift) + (jnp.zeros((depth - channels - 3, width), BF16),)
        qt[channels:, :] = jnp.concatenate([v.astype(F32) for v in parts], axis=0).astype(BF16)

    for p in range(n_block):
        qt[0:channels, p * n_query : (p + 1) * n_query] = query_ref[p].T

    def add_row(i, start):
        for h in range(width // chunk):
            scores = dot(keys[pl.ds(start, tile_cols), :], qt[:, h * chunk : (h + 1) * chunk])
            for l in range(chunk // 128):
                lanes = slice(h * chunk + l * 128, h * chunk + (l + 1) * 128)

                def leaf(g):
                    return jnp.exp2(scores[8 * g : 8 * g + 8, l * 128 : (l + 1) * 128] * scale)

                total, bits = bit_tree(leaf, 0, groups)
                for n, v in enumerate([total, i * total] + bits):
                    acc[n, :, lanes] += v

    def write(shift):
        total, down = acc[0], acc[1]
        along = sum(float(2**b) * acc[2 + b] for b in range(n_bits))
        sub = iota(total.shape, 0).astype(F32)
        first_row = place_ref[0].astype(F32)
        first_col = place_ref[1].astype(F32)
        x = ((2.0 * (first_col + sub) + 1.0) / col_count - 1.0) * total + (16.0 / col_count) * along
        y = ((2.0 * first_row + 1.0) / row_count - 1.0) * total + (2.0 / row_count) * down
        parts = [shift] + [jnp.sum(v, axis=0, keepdims=True) for v in (total, x, y)]
        for p in range(n_block):
            lanes = slice(p * n_query, (p + 1) * n_query)
            block = jnp.concatenate([v[:, lanes] for v in parts], axis=0)
            if second:
                out_ref[p, 1 - place_ref[2]] = block
                out_ref[p, place_ref[2]] = other_ref[p]
            else:
                out_ref[p] = block

    sample = jnp.concatenate(
        [keys[i * tile_cols : i * tile_cols + 16, 0:channels] for i in range(tile_rows)], axis=0
    )
    shift = jnp.max(dot(sample, qt[0:channels, :]), axis=0, keepdims=True)
    set_shift(shift)
    acc[...] = jnp.zeros_like(acc)
    for i in range(tile_rows):
        add_row(float(i), i * tile_cols)
    write(shift)

    @pl.when(jnp.logical_not(jnp.max(acc[0]) < 1e30))
    def _():
        def raise_max(i, top):
            start = pl.multiple_of(i * tile_cols, tile_cols)
            scores = dot(keys[pl.ds(start, tile_cols), 0:channels], qt[0:channels, :])
            return jnp.maximum(top, jnp.max(scores, axis=0, keepdims=True))

        top = lax.fori_loop(0, tile_rows, raise_max, jnp.full((1, width), -jnp.inf, F32))
        set_shift(top)
        acc[...] = jnp.zeros_like(acc)

        def again(i, carry):
            add_row(i.astype(F32), pl.multiple_of(i * tile_cols, tile_cols))
            return carry

        lax.fori_loop(0, tile_rows, again, 0)
        write(top)


def whole(shape):
    return pl.BlockSpec(shape, lambda *_: (0,) * len(shape))


def merged(states, scale):
    highest = jnp.max(states[:, 0], axis=0)
    factor = jnp.exp2((states[:, 0] - highest[None]) * scale)
    sums = jnp.sum(states[:, 1:] * factor[:, None], axis=0)
    return jnp.concatenate([highest[None], sums], axis=0)


def on_device(frame_two, frame_band, conv_weight):
    channels_in, rows_in, cols_in = frame_two.shape
    channels = conv_weight.shape[1]
    tile_rows, tile_cols = rows_in // 2, cols_in // 2
    band_rows, band_cols = (frame_band.shape[1] - 1) // 2, frame_band.shape[2] // 2
    pb = ("chip", "core")
    n_chip, n_pb, n_ka = lax.axis_size("chip"), lax.axis_size(pb), lax.axis_size("ka")
    row_count, col_count = tile_rows * n_pb, tile_cols * n_ka
    pb_index, ka_index = lax.axis_index(pb), lax.axis_index("ka")
    n_query = band_rows * band_cols
    weights = conv_weight.transpose(0, 2, 1)
    params = pltpu.CompilerParams(vmem_limit_bytes=VMEM)

    depth = channels_in * GROUP
    whole_band = (band_rows * 2 + 1, channels_in, 2 * band_cols)
    outs = (
        jax.ShapeDtypeStruct((n_query, channels), BF16),
        jax.ShapeDtypeStruct((2 * band_rows, channels), F32),
        jax.ShapeDtypeStruct((channels_in + 16, cols_in), BF16),
        jax.ShapeDtypeStruct((16, depth), BF16),
    )
    main, edge, down, right = pl.pallas_call(
        query_kernel,
        grid=(1,),
        in_specs=[
            whole(whole_band),
            whole(weights.shape),
            pl.BlockSpec((channels_in, 16, cols_in), lambda i: (0, rows_in // 16 - 1, 0)),
            pl.BlockSpec((channels_in, rows_in, 128), lambda i: (0, 0, cols_in // 128 - 1)),
        ],
        out_specs=[whole(v.shape) for v in outs],
        out_shape=outs,
        compiler_params=params,
        name="query_feats",
    )(frame_band.transpose(1, 0, 2), weights, frame_two, frame_two)
    above = lax.ppermute(down, pb, [(i, i + 1) for i in range(n_pb - 1)])
    copies, right = pl.pallas_call(
        spread_kernel,
        out_shape=(jax.ShapeDtypeStruct((n_chip, n_query, channels), BF16), outs[3]),
        compiler_params=params,
        name="query_copies",
    )(main, edge, above, right)
    side = lax.ppermute(right, "ka", [(i, i + 1) for i in range(n_ka - 1)])
    copies, side = lax.optimization_barrier((copies, side))
    queries = lax.all_to_all(copies, "chip", 0, 0)

    n_key = tile_rows * tile_cols
    keys = pl.pallas_call(
        key_kernel,
        out_shape=jax.ShapeDtypeStruct((n_key, channels + 16), BF16),
        scratch_shapes=[pltpu.VMEM((3, depth, (GROUP // 2 + 1) * channels), BF16)],
        compiler_params=params,
        name="key_feats",
    )(frame_two, weights, above, side)
    queries, keys = lax.optimization_barrier((queries, keys))
    twins = lax.ppermute(queries, "core", [(0, 1), (1, 0)])

    place = jnp.stack(
        [pb_index * tile_rows, ka_index * tile_cols, lax.axis_index("core")]
    ).astype(jnp.int32)
    n_block = 4
    scale = math.log2(math.e) / math.sqrt(channels)

    def attend(block, other):
        ins = [keys]
        in_specs = [
            pl.BlockSpec(memory_space=pltpu.SMEM),
            pl.BlockSpec((n_block, n_query, channels), lambda i: (i, 0, 0)),
        ] + [whole(v.shape) for v in ins]
        if other is None:
            out_spec = pl.BlockSpec((n_block, 4, n_query), lambda i: (i, 0, 0))
            out_shape = (n_chip, 4, n_query)
        else:
            ins.append(other)
            in_specs.append(pl.BlockSpec((n_block, 4, n_query), lambda i: (i, 0, 0)))
            out_spec = pl.BlockSpec((n_block, 2, 4, n_query), lambda i: (i, 0, 0, 0))
            out_shape = (n_chip, 2, 4, n_query)
        return pl.pallas_call(
            functools.partial(
                attention_kernel,
                tile_rows, float(row_count), float(col_count), scale, other is not None,
            ),
            grid=(n_chip // n_block,),
            in_specs=in_specs,
            out_specs=out_spec,
            out_shape=jax.ShapeDtypeStruct(out_shape, F32),
            scratch_shapes=[
                pltpu.VMEM((channels + 16, n_block * n_query), BF16),
                pltpu.VMEM((2 + int(math.log2(tile_cols // 8)), 8, n_block * n_query), F32),
            ],
            compiler_params=params,
            name="attention",
        )(place, block, *ins)

    states = attend(twins, attend(queries, None)).reshape(n_pb, 4, n_query)
    mine = merged(lax.all_to_all(states, pb, 0, 0), scale)
    copies = jnp.broadcast_to(mine[None], (n_ka, 4, n_query))
    final = merged(lax.all_to_all(copies, "ka", 0, 0), scale)
    mean_x = (final[2] / final[1]).reshape(band_rows, band_cols)
    mean_y = (final[3] / final[1]).reshape(band_rows, band_cols)
    query_x = (
        2.0 * (pb_index * band_cols + jnp.arange(band_cols, dtype=jnp.int32)).astype(F32) + 1.0
    ) / col_count - 1.0
    band_top = (row_count - band_rows) // 2
    query_y = (
        2.0 * (band_top + jnp.arange(band_rows, dtype=jnp.int32)).astype(F32) + 1.0
    ) / row_count - 1.0
    return jnp.stack([mean_x - query_x[None, :], mean_y - query_y[:, None]])


def solution(mesh):
    n_pb, n_ka = mesh.shape["pb"], mesh.shape["ka"]
    finer = jax.sharding.Mesh(
        mesh.devices.reshape(n_pb // 2, 2, n_ka), ("chip", "core", "ka")
    )
    pb = ("chip", "core")
    in_specs = (P(None, pb, "ka"), P(None, None, pb), P())
    out_specs = P(None, None, pb)
    return jax.shard_map(
        on_device, mesh=finer, in_specs=in_specs, out_specs=out_specs, check_vma=False
    )
```

```python
import functools
import math

import jax
import jax.numpy as jnp
from jax import lax
from jax.experimental import pallas as pl
from jax.experimental.pallas import tpu as pltpu
from jax.sharding import PartitionSpec as P

BF16 = jnp.bfloat16
F32 = jnp.float32
GROUP = 8
VMEM = 56 * 1024 * 1024


def dot(a, b):
    return jnp.dot(a, b, preferred_element_type=F32)


def dot_nt(a, b):
    return lax.dot_general(a, b, (((1,), (1,)), ((), ())), preferred_element_type=F32)


def iota(shape, axis):
    return lax.broadcasted_iota(jnp.int32, shape, axis)


def tap_selector(cols):
    half = cols // 2
    row = iota((3 * half, cols), 0)
    tap = row // half
    source = 2 * (row - tap * half) - 1 + tap
    return (iota((3 * half, cols), 1) == source).astype(BF16)


def split3(x):
    high = x.astype(BF16)
    rest = x - high.astype(F32)
    mid = rest.astype(BF16)
    low = (rest - mid.astype(F32)).astype(BF16)
    return high, mid, low


def last_lane(x):
    rows, cols = x.shape
    picker = (iota((16, cols), 1) == cols - 1).astype(BF16)
    return dot_nt(picker, x)


def group_of(x_ref, g):
    channels_in, _, cols = x_ref.shape
    base = (g * GROUP) // 16 * 16
    pair = x_ref[:, base : base + 16, :].astype(F32)
    off = g * GROUP - base
    return pair[:, off : off + GROUP, :].reshape(channels_in * GROUP, cols).astype(BF16)


def query_kernel(band_ref, w_ref, bottom_ref, right_ref, out_ref, edge_ref, down_ref, side_ref):
    rows_in, channels_in, cols = band_ref.shape
    rows = (rows_in - 1) // 2
    half = cols // 2
    n_query = rows * half
    channels = w_ref.shape[2]
    selector = tap_selector(cols)
    picked = [dot_nt(selector, band_ref[r]).astype(BF16) for r in range(rows_in)]
    total = jnp.zeros((n_query, channels), F32)
    beyond = jnp.zeros((rows * 16, channels), F32)
    for a in range(3):
        for b in range(3):
            lhs = jnp.concatenate(
                [picked[2 * r + a][b * half : (b + 1) * half] for r in range(rows)], axis=0
            )
            total = total + dot(lhs, w_ref[3 * a + b])
        last = jnp.concatenate(
            [picked[2 * r + a][3 * half - 16 : 3 * half] for r in range(rows)], axis=0
        )
        beyond = beyond + dot(last, w_ref[3 * a])
    out_ref[...] = total.astype(BF16)
    edge_ref[...] = jnp.concatenate(
        [total[r * half : r * half + 1] for r in range(rows)] * 2, axis=0
    )

    depth = channels_in * GROUP
    wide = bottom_ref.shape[2]
    picker = (iota((channels_in, depth), 1) == iota((channels_in, depth), 0) * GROUP + GROUP - 1)
    last_group = bottom_ref.shape[1] // GROUP - 1
    bottom = dot(picker.astype(BF16), group_of(bottom_ref, last_group))
    down_ref[0:channels_in, :] = bottom.astype(BF16)
    ext = jnp.concatenate(
        [beyond[r * 16 + 15 : r * 16 + 16] for r in range(rows)]
        + [jnp.zeros((16 - rows, channels), F32)],
        axis=0,
    )
    parts = [v.astype(F32) for v in split3(ext)]
    blank = jnp.zeros((16, wide - 3 * channels), F32)
    down_ref[channels_in:, :] = jnp.concatenate(parts + [blank], axis=1).astype(BF16)

    side = jnp.zeros((16, depth), F32)
    for g in range(right_ref.shape[1] // GROUP):
        side = jnp.where(iota(side.shape, 0) == g, last_lane(group_of(right_ref, g)), side)
    side_ref[...] = side.astype(BF16)


def join_kernel(main_ref, edge_ref, down_ref, side_ref, out_ref, corner_ref):
    n_query, channels = main_ref.shape
    rows = edge_ref.shape[0] // 2
    half = n_query // rows
    depth = side_ref.shape[1]
    channels_in = depth // GROUP
    wide = down_ref.shape[1]
    tail = down_ref[channels_in:, :].astype(F32)
    before = sum(tail[:, n * channels : (n + 1) * channels] for n in range(3))
    fixed = edge_ref[...] + before[0:8]
    pieces = []
    for r in range(rows):
        old = main_ref[r * half : r * half + 16, :].astype(F32)
        new = jnp.where(
            iota(old.shape, 0) == 0, jnp.broadcast_to(fixed[r : r + 1], old.shape), old
        )
        pieces += [new.astype(BF16), main_ref[r * half + 16 : (r + 1) * half, :]]
    out_ref[...] = jnp.concatenate(pieces, axis=0)
    row = down_ref[0:channels_in, wide - 128 :]
    row = jnp.concatenate([row, jnp.zeros((depth - channels_in, 128), BF16)], axis=0)
    side = side_ref[...].astype(F32)
    corner_ref[...] = jnp.where(iota(side.shape, 0) == 8, last_lane(row), side).astype(BF16)


def key_kernel(x_ref, w_ref, above_ref, side_ref, key_ref, band_ref):
    channels_in, rows_in, cols = x_ref.shape
    half = cols // 2
    channels = w_ref.shape[2]
    depth = channels_in * GROUP
    outs = GROUP // 2
    n_group = rows_in // GROUP
    expand = (iota((depth, channels_in), 0) // GROUP == iota((depth, channels_in), 1)).astype(BF16)
    row = iota((depth, channels), 0) % GROUP
    for b in range(3):
        spread = [dot(expand, w_ref[3 * a + b]) for a in range(3)]
        for i in range(outs + 1):
            block = jnp.zeros((depth, channels), F32)
            for a in range(3):
                block = jnp.where(row == 2 * i - 1 + a, spread[a], block)
            band_ref[b, :, i * channels : (i + 1) * channels] = block.astype(BF16)
    selector = tap_selector(cols)
    side = side_ref[...].astype(F32)

    def taps(x, left):
        picked = dot_nt(selector, x)
        first = picked[0:half]
        first = jnp.where(iota(first.shape, 0) == 0, jnp.broadcast_to(left, first.shape), first)
        return first.astype(BF16), picked[half : 2 * half].astype(BF16), picked[2 * half :].astype(BF16)

    upper = taps(above_ref[0:channels_in, :], side[8:9, 0:channels_in])
    carried = sum(dot(upper[b], w_ref[b]) for b in range(3))
    for g in range(n_group):
        picked = taps(group_of(x_ref, g), side[g : g + 1])
        total = sum(dot(picked[b], band_ref[b]) for b in range(3))
        for i in range(outs):
            part = total[:, i * channels : (i + 1) * channels]
            if i == 0:
                part = part + carried
            o = g * outs + i
            key_ref[o * half : (o + 1) * half, 0:channels] = part.astype(BF16)
        carried = total[:, outs * channels :]
    pad = (key_ref.shape[0], key_ref.shape[1] - channels)
    key_ref[:, channels:] = jnp.where(iota(pad, 1) < 3, -1.0, 0.0).astype(BF16)


def bit_tree(leaf, start, count):
    if count == 1:
        return leaf(start), []
    low, low_bits = bit_tree(leaf, start, count // 2)
    high, high_bits = bit_tree(leaf, start + count // 2, count // 2)
    return low + high, [a + b for a, b in zip(low_bits, high_bits)] + [high]


def attention_kernel(
    tile_rows, row_count, col_count, scale, second,
    place_ref, query_ref, keys, *refs,
):
    if second:
        other_ref, out_ref, qt, acc = refs
    else:
        out_ref, qt, acc = refs
    n_block, n_query, channels = query_ref.shape
    tile_cols = keys.shape[0] // tile_rows
    groups = tile_cols // 8
    n_bits = int(math.log2(groups))
    width = n_block * n_query
    chunk = min(width, 512)
    depth = keys.shape[1]

    def set_shift(shift):
        parts = split3(shift) + (jnp.zeros((depth - channels - 3, width), BF16),)
        qt[channels:, :] = jnp.concatenate([v.astype(F32) for v in parts], axis=0).astype(BF16)

    for p in range(n_block):
        qt[0:channels, p * n_query : (p + 1) * n_query] = query_ref[p].T

    def add_row(i, start):
        for h in range(width // chunk):
            scores = dot(keys[pl.ds(start, tile_cols), :], qt[:, h * chunk : (h + 1) * chunk])
            for l in range(chunk // 128):
                lanes = slice(h * chunk + l * 128, h * chunk + (l + 1) * 128)

                def leaf(g):
                    return jnp.exp2(scores[8 * g : 8 * g + 8, l * 128 : (l + 1) * 128] * scale)

                total, bits = bit_tree(leaf, 0, groups)
                for n, v in enumerate([total, i * total] + bits):
                    acc[n, :, lanes] += v

    def write(shift):
        total, down = acc[0], acc[1]
        along = sum(float(2**b) * acc[2 + b] for b in range(n_bits))
        sub = iota(total.shape, 0).astype(F32)
        first_row = place_ref[0].astype(F32)
        first_col = place_ref[1].astype(F32)
        x = ((2.0 * (first_col + sub) + 1.0) / col_count - 1.0) * total + (16.0 / col_count) * along
        y = ((2.0 * first_row + 1.0) / row_count - 1.0) * total + (2.0 / row_count) * down
        parts = [shift] + [jnp.sum(v, axis=0, keepdims=True) for v in (total, x, y)]
        for p in range(n_block):
            lanes = slice(p * n_query, (p + 1) * n_query)
            block = jnp.concatenate([v[:, lanes] for v in parts], axis=0)
            there = (place_ref[3] + n_block - p) % n_block
            if second:
                out_ref[there, 1 - place_ref[2]] = block
                out_ref[p, place_ref[2]] = other_ref[p]
            else:
                out_ref[there] = block

    sample = jnp.concatenate(
        [keys[i * tile_cols : i * tile_cols + 16, 0:channels] for i in range(tile_rows)], axis=0
    )
    shift = jnp.max(dot(sample, qt[0:channels, :]), axis=0, keepdims=True)
    set_shift(shift)
    acc[...] = jnp.zeros_like(acc)
    for i in range(tile_rows):
        add_row(float(i), i * tile_cols)
    write(shift)

    @pl.when(jnp.logical_not(jnp.max(acc[0]) < 1e30))
    def _():
        def raise_max(i, top):
            start = pl.multiple_of(i * tile_cols, tile_cols)
            scores = dot(keys[pl.ds(start, tile_cols), 0:channels], qt[0:channels, :])
            return jnp.maximum(top, jnp.max(scores, axis=0, keepdims=True))

        top = lax.fori_loop(0, tile_rows, raise_max, jnp.full((1, width), -jnp.inf, F32))
        set_shift(top)
        acc[...] = jnp.zeros_like(acc)

        def again(i, carry):
            add_row(i.astype(F32), pl.multiple_of(i * tile_cols, tile_cols))
            return carry

        lax.fori_loop(0, tile_rows, again, 0)
        write(top)


def whole(shape):
    return pl.BlockSpec(shape, lambda *_: (0,) * len(shape))


def merged(states, scale):
    highest = jnp.max(states[:, 0], axis=0)
    factor = jnp.exp2((states[:, 0] - highest[None]) * scale)
    sums = jnp.sum(states[:, 1:] * factor[:, None], axis=0)
    return jnp.concatenate([highest[None], sums], axis=0)


def on_device(frame_two, frame_band, conv_weight):
    channels_in, rows_in, cols_in = frame_two.shape
    channels = conv_weight.shape[1]
    tile_rows, tile_cols = rows_in // 2, cols_in // 2
    band_rows, band_cols = (frame_band.shape[1] - 1) // 2, frame_band.shape[2] // 2
    pb = ("x", "z", "core")
    n_chip, n_pb, n_ka = lax.axis_size(("x", "z")), lax.axis_size(pb), lax.axis_size("ka")
    row_count, col_count = tile_rows * n_pb, tile_cols * n_ka
    pb_index, ka_index = lax.axis_index(pb), lax.axis_index("ka")
    n_query = band_rows * band_cols
    weights = conv_weight.transpose(0, 2, 1)
    params = pltpu.CompilerParams(vmem_limit_bytes=VMEM)

    depth = channels_in * GROUP
    whole_band = (band_rows * 2 + 1, channels_in, 2 * band_cols)
    outs = (
        jax.ShapeDtypeStruct((n_query, channels), BF16),
        jax.ShapeDtypeStruct((2 * band_rows, channels), F32),
        jax.ShapeDtypeStruct((channels_in + 16, cols_in), BF16),
        jax.ShapeDtypeStruct((16, depth), BF16),
    )
    main, edge, down, right = pl.pallas_call(
        query_kernel,
        grid=(1,),
        in_specs=[
            whole(whole_band),
            whole(weights.shape),
            pl.BlockSpec((channels_in, 16, cols_in), lambda i: (0, rows_in // 16 - 1, 0)),
            pl.BlockSpec((channels_in, rows_in, 128), lambda i: (0, 0, cols_in // 128 - 1)),
        ],
        out_specs=[whole(v.shape) for v in outs],
        out_shape=outs,
        compiler_params=params,
        name="query_feats",
    )(frame_band.transpose(1, 0, 2), weights, frame_two, frame_two)
    above = lax.ppermute(down, pb, [(i, i + 1) for i in range(n_pb - 1)])
    mine, right = pl.pallas_call(
        join_kernel,
        out_shape=(outs[0], outs[3]),
        compiler_params=params,
        name="query_join",
    )(main, edge, above, right)
    side = lax.ppermute(right, "ka", [(i, i + 1) for i in range(n_ka - 1)])

    def circled(x, axis):
        count = lax.axis_size(axis)
        turns = [[(i, (i + d) % count) for i in range(count)] for d in range(1, count)]
        return jnp.stack([x] + [lax.ppermute(x, axis, pairs) for pairs in turns])

    near, side = lax.optimization_barrier((circled(mine, "z"), side))
    queries = circled(near, "x").reshape(n_chip, n_query, channels)

    n_key = tile_rows * tile_cols
    keys = pl.pallas_call(
        key_kernel,
        out_shape=jax.ShapeDtypeStruct((n_key, channels + 16), BF16),
        scratch_shapes=[pltpu.VMEM((3, depth, (GROUP // 2 + 1) * channels), BF16)],
        compiler_params=params,
        name="key_feats",
    )(frame_two, weights, above, side)
    queries, keys = lax.optimization_barrier((queries, keys))
    twins = lax.ppermute(queries, "core", [(0, 1), (1, 0)])

    place = jnp.stack(
        [
            pb_index * tile_rows,
            ka_index * tile_cols,
            lax.axis_index("core"),
            lax.axis_index("z"),
            lax.axis_index("x"),
        ]
    ).astype(jnp.int32)
    n_block, n_x = lax.axis_size("z"), lax.axis_size("x")
    scale = math.log2(math.e) / math.sqrt(channels)

    def attend(block, other):
        def there(i, place):
            return (place[4] + n_x - i) % n_x

        ins = [keys]
        in_specs = [
            pl.BlockSpec((n_block, n_query, channels), lambda i, place: (i, 0, 0)),
            whole(keys.shape),
        ]
        if other is None:
            out_spec = pl.BlockSpec(
                (n_block, 4, n_query), lambda i, place: (there(i, place), 0, 0)
            )
            out_shape = (n_chip, 4, n_query)
        else:
            ins.append(other)
            in_specs.append(
                pl.BlockSpec((n_block, 4, n_query), lambda i, place: (there(i, place), 0, 0))
            )
            out_spec = pl.BlockSpec(
                (n_block, 2, 4, n_query), lambda i, place: (there(i, place), 0, 0, 0)
            )
            out_shape = (n_chip, 2, 4, n_query)
        return pl.pallas_call(
            functools.partial(
                attention_kernel,
                tile_rows, float(row_count), float(col_count), scale, other is not None,
            ),
            grid_spec=pltpu.PrefetchScalarGridSpec(
                num_scalar_prefetch=1,
                grid=(n_x,),
                in_specs=in_specs,
                out_specs=out_spec,
                scratch_shapes=[
                    pltpu.VMEM((channels + 16, n_block * n_query), BF16),
                    pltpu.VMEM((2 + int(math.log2(tile_cols // 8)), 8, n_block * n_query), F32),
                ],
            ),
            out_shape=jax.ShapeDtypeStruct(out_shape, F32),
            compiler_params=params,
            name="attention",
        )(place, block, *ins)

    states = attend(twins, attend(queries, None)).reshape(n_pb, 4, n_query)
    mine = merged(lax.all_to_all(states, pb, 0, 0), scale)
    copies = jnp.broadcast_to(mine[None], (n_ka, 4, n_query))
    final = merged(lax.all_to_all(copies, "ka", 0, 0), scale)
    mean_x = (final[2] / final[1]).reshape(band_rows, band_cols)
    mean_y = (final[3] / final[1]).reshape(band_rows, band_cols)
    query_x = (
        2.0 * (pb_index * band_cols + jnp.arange(band_cols, dtype=jnp.int32)).astype(F32) + 1.0
    ) / col_count - 1.0
    band_top = (row_count - band_rows) // 2
    query_y = (
        2.0 * (band_top + jnp.arange(band_rows, dtype=jnp.int32)).astype(F32) + 1.0
    ) / row_count - 1.0
    return jnp.stack([mean_x - query_x[None, :], mean_y - query_y[:, None]])


def solution(mesh):
    n_pb, n_ka = mesh.shape["pb"], mesh.shape["ka"]
    finer = jax.sharding.Mesh(
        mesh.devices.reshape(n_pb // 8, 4, 2, n_ka), ("x", "z", "core", "ka")
    )
    pb = ("x", "z", "core")
    in_specs = (P(None, pb, "ka"), P(None, None, pb), P())
    out_specs = P(None, None, pb)
    return jax.shard_map(
        on_device, mesh=finer, in_specs=in_specs, out_specs=out_specs, check_vma=False
    )
```

```python
import functools
import math

import jax
import jax.numpy as jnp
from jax import lax
from jax.experimental import pallas as pl
from jax.experimental.pallas import tpu as pltpu
from jax.sharding import PartitionSpec as P

BF16 = jnp.bfloat16
F32 = jnp.float32
GROUP = 8
VMEM = 56 * 1024 * 1024


def dot(a, b):
    return jnp.dot(a, b, preferred_element_type=F32)


def dot_nt(a, b):
    return lax.dot_general(a, b, (((1,), (1,)), ((), ())), preferred_element_type=F32)


def iota(shape, axis):
    return lax.broadcasted_iota(jnp.int32, shape, axis)


def tap_selector(cols):
    half = cols // 2
    row = iota((3 * half, cols), 0)
    tap = row // half
    source = 2 * (row - tap * half) - 1 + tap
    return (iota((3 * half, cols), 1) == source).astype(BF16)


def split3(x):
    high = x.astype(BF16)
    rest = x - high.astype(F32)
    mid = rest.astype(BF16)
    low = (rest - mid.astype(F32)).astype(BF16)
    return high, mid, low


def last_lane(x):
    rows, cols = x.shape
    picker = (iota((16, cols), 1) == cols - 1).astype(BF16)
    return dot_nt(picker, x)


def group_of(x_ref, g):
    channels_in, _, cols = x_ref.shape
    base = (g * GROUP) // 16 * 16
    pair = x_ref[:, base : base + 16, :].astype(F32)
    off = g * GROUP - base
    return pair[:, off : off + GROUP, :].reshape(channels_in * GROUP, cols).astype(BF16)


def query_kernel(band_ref, w_ref, bottom_ref, right_ref, out_ref, edge_ref, down_ref, side_ref):
    rows_in, channels_in, cols = band_ref.shape
    rows = (rows_in - 1) // 2
    half = cols // 2
    n_query = rows * half
    channels = w_ref.shape[2]
    selector = tap_selector(cols)
    picked = [dot_nt(selector, band_ref[r]).astype(BF16) for r in range(rows_in)]
    total = jnp.zeros((n_query, channels), F32)
    beyond = jnp.zeros((rows * 16, channels), F32)
    for a in range(3):
        for b in range(3):
            lhs = jnp.concatenate(
                [picked[2 * r + a][b * half : (b + 1) * half] for r in range(rows)], axis=0
            )
            total = total + dot(lhs, w_ref[3 * a + b])
        last = jnp.concatenate(
            [picked[2 * r + a][3 * half - 16 : 3 * half] for r in range(rows)], axis=0
        )
        beyond = beyond + dot(last, w_ref[3 * a])
    out_ref[...] = total.astype(BF16)
    edge_ref[...] = jnp.concatenate(
        [total[r * half : r * half + 1] for r in range(rows)] * 2, axis=0
    )

    depth = channels_in * GROUP
    wide = bottom_ref.shape[2]
    picker = (iota((channels_in, depth), 1) == iota((channels_in, depth), 0) * GROUP + GROUP - 1)
    last_group = bottom_ref.shape[1] // GROUP - 1
    bottom = dot(picker.astype(BF16), group_of(bottom_ref, last_group))
    down_ref[0:channels_in, :] = bottom.astype(BF16)
    ext = jnp.concatenate(
        [beyond[r * 16 + 15 : r * 16 + 16] for r in range(rows)]
        + [jnp.zeros((16 - rows, channels), F32)],
        axis=0,
    )
    parts = [v.astype(F32) for v in split3(ext)]
    blank = jnp.zeros((16, wide - 3 * channels), F32)
    down_ref[channels_in:, :] = jnp.concatenate(parts + [blank], axis=1).astype(BF16)

    side = jnp.zeros((16, depth), F32)
    for g in range(right_ref.shape[1] // GROUP):
        side = jnp.where(iota(side.shape, 0) == g, last_lane(group_of(right_ref, g)), side)
    side_ref[...] = side.astype(BF16)


def join_kernel(main_ref, edge_ref, down_ref, side_ref, out_ref, corner_ref):
    n_query, channels = main_ref.shape
    rows = edge_ref.shape[0] // 2
    half = n_query // rows
    depth = side_ref.shape[1]
    channels_in = depth // GROUP
    wide = down_ref.shape[1]
    tail = down_ref[channels_in:, :].astype(F32)
    before = sum(tail[:, n * channels : (n + 1) * channels] for n in range(3))
    fixed = edge_ref[...] + before[0:8]
    pieces = []
    for r in range(rows):
        old = main_ref[r * half : r * half + 16, :].astype(F32)
        new = jnp.where(
            iota(old.shape, 0) == 0, jnp.broadcast_to(fixed[r : r + 1], old.shape), old
        )
        pieces += [new.astype(BF16), main_ref[r * half + 16 : (r + 1) * half, :]]
    out_ref[...] = jnp.concatenate(pieces, axis=0)
    row = down_ref[0:channels_in, wide - 128 :]
    row = jnp.concatenate([row, jnp.zeros((depth - channels_in, 128), BF16)], axis=0)
    side = side_ref[...].astype(F32)
    corner_ref[...] = jnp.where(iota(side.shape, 0) == 8, last_lane(row), side).astype(BF16)


def weight_kernel(w_ref, band_ref):
    _, depth, wide = band_ref.shape
    _, channels_in, channels = w_ref.shape
    expand = (iota((depth, channels_in), 0) // GROUP == iota((depth, channels_in), 1)).astype(BF16)
    row = iota((depth, channels), 0) % GROUP
    for b in range(3):
        spread = [dot(expand, w_ref[3 * a + b]) for a in range(3)]
        for i in range(wide // channels):
            block = jnp.zeros((depth, channels), F32)
            for a in range(3):
                block = jnp.where(row == 2 * i - 1 + a, spread[a], block)
            band_ref[b, :, i * channels : (i + 1) * channels] = block.astype(BF16)


def key_kernel(x_ref, w_ref, band_ref, above_ref, side_ref, key_ref):
    channels_in, rows_in, cols = x_ref.shape
    half = cols // 2
    channels = w_ref.shape[2]
    outs = GROUP // 2
    n_group = rows_in // GROUP
    block = min(cols, 256)
    place = iota((block, block), 0)
    parity = place // (block // 2)
    source = 2 * (place - parity * (block // 2)) + parity
    selector = (iota((block, block), 1) == source).astype(BF16)
    side = side_ref[...].astype(F32)

    def taps(x, left):
        picked = [dot_nt(selector, x[:, c : c + block]) for c in range(0, cols, block)]
        even = jnp.concatenate([v[0 : block // 2] for v in picked], axis=0)
        odd = jnp.concatenate([v[block // 2 :] for v in picked], axis=0)
        first = pltpu.roll(odd, 1, 0)
        first = jnp.where(iota(first.shape, 0) == 0, jnp.broadcast_to(left, first.shape), first)
        return first.astype(BF16), even.astype(BF16), odd.astype(BF16)

    upper = taps(above_ref[0:channels_in, :], side[8:9, 0:channels_in])
    carried = sum(dot(upper[b], w_ref[b]) for b in range(3))
    for g in range(n_group):
        picked = taps(group_of(x_ref, g), side[g : g + 1])
        total = sum(dot(picked[b], band_ref[b]) for b in range(3))
        for i in range(outs):
            part = total[:, i * channels : (i + 1) * channels]
            if i == 0:
                part = part + carried
            o = g * outs + i
            key_ref[o * half : (o + 1) * half, 0:channels] = part.astype(BF16)
        carried = total[:, outs * channels :]
    pad = (key_ref.shape[0], key_ref.shape[1] - channels)
    key_ref[:, channels:] = jnp.where(iota(pad, 1) < 3, -1.0, 0.0).astype(BF16)


def bit_tree(leaf, start, count):
    if count == 1:
        return leaf(start), []
    low, low_bits = bit_tree(leaf, start, count // 2)
    high, high_bits = bit_tree(leaf, start + count // 2, count // 2)
    return low + high, [a + b for a, b in zip(low_bits, high_bits)] + [high]


def attention_kernel(
    tile_rows, row_count, col_count, scale, second,
    place_ref, query_ref, keys, *refs,
):
    if second:
        other_ref, out_ref, qt, acc = refs
    else:
        out_ref, qt, acc = refs
    n_block, n_query, channels = query_ref.shape
    tile_cols = keys.shape[0] // tile_rows
    groups = tile_cols // 8
    n_bits = int(math.log2(groups))
    width = n_block * n_query
    chunk = min(width, 512)
    depth = keys.shape[1]

    def set_shift(shift):
        parts = split3(shift) + (jnp.zeros((depth - channels - 3, width), BF16),)
        qt[channels:, :] = jnp.concatenate([v.astype(F32) for v in parts], axis=0).astype(BF16)

    for p in range(n_block):
        qt[0:channels, p * n_query : (p + 1) * n_query] = query_ref[p].T

    def add_row(i, start):
        for h in range(width // chunk):
            scores = dot(keys[pl.ds(start, tile_cols), :], qt[:, h * chunk : (h + 1) * chunk])
            for l in range(chunk // 128):
                lanes = slice(h * chunk + l * 128, h * chunk + (l + 1) * 128)

                def leaf(g):
                    return jnp.exp2(scores[8 * g : 8 * g + 8, l * 128 : (l + 1) * 128] * scale)

                total, bits = bit_tree(leaf, 0, groups)
                for n, v in enumerate([total, i * total] + bits):
                    acc[n, :, lanes] += v

    def write(shift):
        total, down = acc[0], acc[1]
        along = sum(float(2**b) * acc[2 + b] for b in range(n_bits))
        sub = iota(total.shape, 0).astype(F32)
        first_row = place_ref[0].astype(F32)
        first_col = place_ref[1].astype(F32)
        x = ((2.0 * (first_col + sub) + 1.0) / col_count - 1.0) * total + (16.0 / col_count) * along
        y = ((2.0 * first_row + 1.0) / row_count - 1.0) * total + (2.0 / row_count) * down
        parts = [shift] + [jnp.sum(v, axis=0, keepdims=True) for v in (total, x, y)]
        for p in range(n_block):
            lanes = slice(p * n_query, (p + 1) * n_query)
            block = jnp.concatenate([v[:, lanes] for v in parts], axis=0)
            there = (place_ref[3] + n_block - p) % n_block
            if second:
                out_ref[there, 1 - place_ref[2]] = block
                out_ref[p, place_ref[2]] = other_ref[p]
            else:
                out_ref[there] = block

    sample = jnp.concatenate(
        [keys[i * tile_cols : i * tile_cols + 16, 0:channels] for i in range(tile_rows)], axis=0
    )
    shift = jnp.max(dot(sample, qt[0:channels, :]), axis=0, keepdims=True)
    set_shift(shift)
    acc[...] = jnp.zeros_like(acc)
    for i in range(tile_rows):
        add_row(float(i), i * tile_cols)
    write(shift)

    @pl.when(jnp.logical_not(jnp.max(acc[0]) < 1e30))
    def _():
        def raise_max(i, top):
            start = pl.multiple_of(i * tile_cols, tile_cols)
            scores = dot(keys[pl.ds(start, tile_cols), 0:channels], qt[0:channels, :])
            return jnp.maximum(top, jnp.max(scores, axis=0, keepdims=True))

        top = lax.fori_loop(0, tile_rows, raise_max, jnp.full((1, width), -jnp.inf, F32))
        set_shift(top)
        acc[...] = jnp.zeros_like(acc)

        def again(i, carry):
            add_row(i.astype(F32), pl.multiple_of(i * tile_cols, tile_cols))
            return carry

        lax.fori_loop(0, tile_rows, again, 0)
        write(top)


def whole(shape):
    return pl.BlockSpec(shape, lambda *_: (0,) * len(shape))


def merged(states, scale):
    highest = jnp.max(states[:, 0], axis=0)
    factor = jnp.exp2((states[:, 0] - highest[None]) * scale)
    sums = jnp.sum(states[:, 1:] * factor[:, None], axis=0)
    return jnp.concatenate([highest[None], sums], axis=0)


def on_device(frame_two, frame_band, conv_weight):
    channels_in, rows_in, cols_in = frame_two.shape
    channels = conv_weight.shape[1]
    tile_rows, tile_cols = rows_in // 2, cols_in // 2
    band_rows, band_cols = (frame_band.shape[1] - 1) // 2, frame_band.shape[2] // 2
    pb = ("x", "z", "core")
    n_chip, n_pb, n_ka = lax.axis_size(("x", "z")), lax.axis_size(pb), lax.axis_size("ka")
    row_count, col_count = tile_rows * n_pb, tile_cols * n_ka
    pb_index, ka_index = lax.axis_index(pb), lax.axis_index("ka")
    n_query = band_rows * band_cols
    weights = conv_weight.transpose(0, 2, 1)
    params = pltpu.CompilerParams(vmem_limit_bytes=VMEM)

    depth = channels_in * GROUP
    whole_band = (band_rows * 2 + 1, channels_in, 2 * band_cols)
    outs = (
        jax.ShapeDtypeStruct((n_query, channels), BF16),
        jax.ShapeDtypeStruct((2 * band_rows, channels), F32),
        jax.ShapeDtypeStruct((channels_in + 16, cols_in), BF16),
        jax.ShapeDtypeStruct((16, depth), BF16),
    )
    main, edge, down, right = pl.pallas_call(
        query_kernel,
        grid=(1,),
        in_specs=[
            whole(whole_band),
            whole(weights.shape),
            pl.BlockSpec((channels_in, 16, cols_in), lambda i: (0, rows_in // 16 - 1, 0)),
            pl.BlockSpec((channels_in, rows_in, 128), lambda i: (0, 0, cols_in // 128 - 1)),
        ],
        out_specs=[whole(v.shape) for v in outs],
        out_shape=outs,
        compiler_params=params,
        name="query_feats",
    )(frame_band.transpose(1, 0, 2), weights, frame_two, frame_two)
    above = lax.ppermute(down, pb, [(i, i + 1) for i in range(n_pb - 1)])
    later, edge = lax.optimization_barrier((weights, edge))
    bands = pl.pallas_call(
        weight_kernel,
        out_shape=jax.ShapeDtypeStruct((3, depth, (GROUP // 2 + 1) * channels), BF16),
        compiler_params=params,
        name="key_weights",
    )(later)
    main, bands = lax.optimization_barrier((main, bands))
    mine, right = pl.pallas_call(
        join_kernel,
        out_shape=(outs[0], outs[3]),
        compiler_params=params,
        name="query_join",
    )(main, edge, above, right)
    side = lax.ppermute(right, "ka", [(i, i + 1) for i in range(n_ka - 1)])

    def circled(x, axis):
        count = lax.axis_size(axis)
        turns = [[(i, (i + d) % count) for i in range(count)] for d in range(1, count)]
        return jnp.stack([x] + [lax.ppermute(x, axis, pairs) for pairs in turns])

    near, side = lax.optimization_barrier((circled(mine, "z"), side))
    queries = circled(near, "x").reshape(n_chip, n_query, channels)

    n_key = tile_rows * tile_cols
    keys = pl.pallas_call(
        key_kernel,
        out_shape=jax.ShapeDtypeStruct((n_key, channels + 16), BF16),
        compiler_params=params,
        name="key_feats",
    )(frame_two, weights, bands, above, side)
    queries, keys = lax.optimization_barrier((queries, keys))
    twins = lax.ppermute(queries, "core", [(0, 1), (1, 0)])

    place = jnp.stack(
        [
            pb_index * tile_rows,
            ka_index * tile_cols,
            lax.axis_index("core"),
            lax.axis_index("z"),
            lax.axis_index("x"),
        ]
    ).astype(jnp.int32)
    n_block, n_x = lax.axis_size("z"), lax.axis_size("x")
    scale = math.log2(math.e) / math.sqrt(channels)

    def attend(block, other):
        def there(i, place):
            return (place[4] + n_x - i) % n_x

        ins = [keys]
        in_specs = [
            pl.BlockSpec((n_block, n_query, channels), lambda i, place: (i, 0, 0)),
            whole(keys.shape),
        ]
        if other is None:
            out_spec = pl.BlockSpec(
                (n_block, 4, n_query), lambda i, place: (there(i, place), 0, 0)
            )
            out_shape = (n_chip, 4, n_query)
        else:
            ins.append(other)
            in_specs.append(
                pl.BlockSpec((n_block, 4, n_query), lambda i, place: (there(i, place), 0, 0))
            )
            out_spec = pl.BlockSpec(
                (n_block, 2, 4, n_query), lambda i, place: (there(i, place), 0, 0, 0)
            )
            out_shape = (n_chip, 2, 4, n_query)
        return pl.pallas_call(
            functools.partial(
                attention_kernel,
                tile_rows, float(row_count), float(col_count), scale, other is not None,
            ),
            grid_spec=pltpu.PrefetchScalarGridSpec(
                num_scalar_prefetch=1,
                grid=(n_x,),
                in_specs=in_specs,
                out_specs=out_spec,
                scratch_shapes=[
                    pltpu.VMEM((channels + 16, n_block * n_query), BF16),
                    pltpu.VMEM((2 + int(math.log2(tile_cols // 8)), 8, n_block * n_query), F32),
                ],
            ),
            out_shape=jax.ShapeDtypeStruct(out_shape, F32),
            compiler_params=params,
            name="attention",
        )(place, block, *ins)

    states = attend(twins, attend(queries, None)).reshape(n_pb, 4, n_query)
    mine = merged(lax.all_to_all(states, pb, 0, 0), scale)
    copies = jnp.broadcast_to(mine[None], (n_ka, 4, n_query))
    final = merged(lax.all_to_all(copies, "ka", 0, 0), scale)
    mean_x = (final[2] / final[1]).reshape(band_rows, band_cols)
    mean_y = (final[3] / final[1]).reshape(band_rows, band_cols)
    query_x = (
        2.0 * (pb_index * band_cols + jnp.arange(band_cols, dtype=jnp.int32)).astype(F32) + 1.0
    ) / col_count - 1.0
    band_top = (row_count - band_rows) // 2
    query_y = (
        2.0 * (band_top + jnp.arange(band_rows, dtype=jnp.int32)).astype(F32) + 1.0
    ) / row_count - 1.0
    return jnp.stack([mean_x - query_x[None, :], mean_y - query_y[:, None]])


def solution(mesh):
    n_pb, n_ka = mesh.shape["pb"], mesh.shape["ka"]
    finer = jax.sharding.Mesh(
        mesh.devices.reshape(n_pb // 8, 4, 2, n_ka), ("x", "z", "core", "ka")
    )
    pb = ("x", "z", "core")
    in_specs = (P(None, pb, "ka"), P(None, None, pb), P())
    out_specs = P(None, None, pb)
    return jax.shard_map(
        on_device, mesh=finer, in_specs=in_specs, out_specs=out_specs, check_vma=False
    )
```

```python
import functools
import math

import jax
import jax.numpy as jnp
from jax import lax
from jax.experimental import pallas as pl
from jax.experimental.pallas import tpu as pltpu
from jax.sharding import PartitionSpec as P

BF16 = jnp.bfloat16
F32 = jnp.float32
GROUP = 8
VMEM = 56 * 1024 * 1024


def dot(a, b):
    return jnp.dot(a, b, preferred_element_type=F32)


def dot_nt(a, b):
    return lax.dot_general(a, b, (((1,), (1,)), ((), ())), preferred_element_type=F32)


def iota(shape, axis):
    return lax.broadcasted_iota(jnp.int32, shape, axis)


def tap_selector(cols):
    half = cols // 2
    row = iota((3 * half, cols), 0)
    tap = row // half
    source = 2 * (row - tap * half) - 1 + tap
    return (iota((3 * half, cols), 1) == source).astype(BF16)


def split3(x):
    high = x.astype(BF16)
    rest = x - high.astype(F32)
    mid = rest.astype(BF16)
    low = (rest - mid.astype(F32)).astype(BF16)
    return high, mid, low


def last_lane(x):
    rows, cols = x.shape
    picker = (iota((16, cols), 1) == cols - 1).astype(BF16)
    return dot_nt(picker, x)


def group_of(x_ref, g):
    channels_in, _, cols = x_ref.shape
    base = (g * GROUP) // 16 * 16
    pair = x_ref[:, base : base + 16, :].astype(F32)
    off = g * GROUP - base
    return pair[:, off : off + GROUP, :].reshape(channels_in * GROUP, cols).astype(BF16)


def query_kernel(band_ref, w_ref, bottom_ref, right_ref, out_ref, edge_ref, down_ref, side_ref):
    rows_in, channels_in, cols = band_ref.shape
    rows = (rows_in - 1) // 2
    half = cols // 2
    n_query = rows * half
    channels = w_ref.shape[2]
    selector = tap_selector(cols)
    picked = [dot_nt(selector, band_ref[r]).astype(BF16) for r in range(rows_in)]
    total = jnp.zeros((n_query, channels), F32)
    beyond = jnp.zeros((rows * 16, channels), F32)
    for a in range(3):
        for b in range(3):
            lhs = jnp.concatenate(
                [picked[2 * r + a][b * half : (b + 1) * half] for r in range(rows)], axis=0
            )
            total = total + dot(lhs, w_ref[3 * a + b])
        last = jnp.concatenate(
            [picked[2 * r + a][3 * half - 16 : 3 * half] for r in range(rows)], axis=0
        )
        beyond = beyond + dot(last, w_ref[3 * a])
    out_ref[...] = total.astype(BF16)
    edge_ref[...] = jnp.concatenate(
        [total[r * half : r * half + 1] for r in range(rows)] * 2, axis=0
    )

    depth = channels_in * GROUP
    wide = bottom_ref.shape[2]
    picker = (iota((channels_in, depth), 1) == iota((channels_in, depth), 0) * GROUP + GROUP - 1)
    last_group = bottom_ref.shape[1] // GROUP - 1
    bottom = dot(picker.astype(BF16), group_of(bottom_ref, last_group))
    down_ref[0:channels_in, :] = bottom.astype(BF16)
    ext = jnp.concatenate(
        [beyond[r * 16 + 15 : r * 16 + 16] for r in range(rows)]
        + [jnp.zeros((16 - rows, channels), F32)],
        axis=0,
    )
    parts = [v.astype(F32) for v in split3(ext)]
    blank = jnp.zeros((16, wide - 3 * channels), F32)
    down_ref[channels_in:, :] = jnp.concatenate(parts + [blank], axis=1).astype(BF16)

    side = jnp.zeros((16, depth), F32)
    for g in range(right_ref.shape[1] // GROUP):
        side = jnp.where(iota(side.shape, 0) == g, last_lane(group_of(right_ref, g)), side)
    side_ref[...] = side.astype(BF16)


def join_kernel(main_ref, edge_ref, down_ref, side_ref, out_ref, corner_ref):
    n_query, channels = main_ref.shape
    rows = edge_ref.shape[0] // 2
    half = n_query // rows
    depth = side_ref.shape[1]
    channels_in = depth // GROUP
    wide = down_ref.shape[1]
    tail = down_ref[channels_in:, :].astype(F32)
    before = sum(tail[:, n * channels : (n + 1) * channels] for n in range(3))
    fixed = edge_ref[...] + before[0:8]
    pieces = []
    for r in range(rows):
        old = main_ref[r * half : r * half + 16, :].astype(F32)
        new = jnp.where(
            iota(old.shape, 0) == 0, jnp.broadcast_to(fixed[r : r + 1], old.shape), old
        )
        pieces += [new.astype(BF16), main_ref[r * half + 16 : (r + 1) * half, :]]
    out_ref[...] = jnp.concatenate(pieces, axis=0)
    row = down_ref[0:channels_in, wide - 128 :]
    row = jnp.concatenate([row, jnp.zeros((depth - channels_in, 128), BF16)], axis=0)
    side = side_ref[...].astype(F32)
    corner_ref[...] = jnp.where(iota(side.shape, 0) == 8, last_lane(row), side).astype(BF16)


def weight_kernel(w_ref, band_ref):
    _, depth, wide = band_ref.shape
    _, channels_in, channels = w_ref.shape
    expand = (iota((depth, channels_in), 0) // GROUP == iota((depth, channels_in), 1)).astype(BF16)
    row = iota((depth, channels), 0) % GROUP
    for b in range(3):
        spread = [dot(expand, w_ref[3 * a + b]) for a in range(3)]
        for i in range(wide // channels):
            block = jnp.zeros((depth, channels), F32)
            for a in range(3):
                block = jnp.where(row == 2 * i - 1 + a, spread[a], block)
            band_ref[b, :, i * channels : (i + 1) * channels] = block.astype(BF16)


def key_kernel(x_ref, w_ref, band_ref, above_ref, side_ref, key_ref):
    channels_in, rows_in, cols = x_ref.shape
    half = cols // 2
    channels = w_ref.shape[2]
    outs = GROUP // 2
    n_group = rows_in // GROUP
    block = min(cols, 256)
    place = iota((block, block), 0)
    parity = place // (block // 2)
    source = 2 * (place - parity * (block // 2)) + parity
    selector = (iota((block, block), 1) == source).astype(BF16)
    side = side_ref[...].astype(F32)

    def taps(x, left):
        picked = [dot_nt(selector, x[:, c : c + block]) for c in range(0, cols, block)]
        even = jnp.concatenate([v[0 : block // 2] for v in picked], axis=0)
        odd = jnp.concatenate([v[block // 2 :] for v in picked], axis=0)
        first = pltpu.roll(odd, 1, 0)
        first = jnp.where(iota(first.shape, 0) == 0, jnp.broadcast_to(left, first.shape), first)
        return first.astype(BF16), even.astype(BF16), odd.astype(BF16)

    upper = taps(above_ref[0:channels_in, :], side[8:9, 0:channels_in])
    carried = sum(dot(upper[b], w_ref[b]) for b in range(3))
    for g in range(n_group):
        picked = taps(group_of(x_ref, g), side[g : g + 1])
        total = sum(dot(picked[b], band_ref[b]) for b in range(3))
        for i in range(outs):
            part = total[:, i * channels : (i + 1) * channels]
            if i == 0:
                part = part + carried
            o = g * outs + i
            key_ref[o * half : (o + 1) * half, 0:channels] = part.astype(BF16)
        carried = total[:, outs * channels :]
    pad = (key_ref.shape[0], key_ref.shape[1] - channels)
    key_ref[:, channels:] = jnp.where(iota(pad, 1) < 3, -1.0, 0.0).astype(BF16)


def bit_tree(leaf, start, count):
    if count == 1:
        return leaf(start), []
    low, low_bits = bit_tree(leaf, start, count // 2)
    high, high_bits = bit_tree(leaf, start + count // 2, count // 2)
    return low + high, [a + b for a, b in zip(low_bits, high_bits)] + [high]


def attention_kernel(
    tile_rows, row_count, col_count, scale, second,
    place_ref, query_ref, keys, *refs,
):
    if second:
        other_ref, out_ref, qt, acc = refs
    else:
        out_ref, qt, acc = refs
    n_block, n_query, channels = query_ref.shape
    tile_cols = keys.shape[0] // tile_rows
    groups = tile_cols // 8
    n_bits = int(math.log2(groups))
    width = n_block * n_query
    chunk = min(width, 512)
    depth = keys.shape[1]

    def set_shift(shift):
        parts = split3(shift) + (jnp.zeros((depth - channels - 3, width), BF16),)
        qt[channels:, :] = jnp.concatenate([v.astype(F32) for v in parts], axis=0).astype(BF16)

    for p in range(n_block):
        qt[0:channels, p * n_query : (p + 1) * n_query] = query_ref[p].T

    def add_row(i, start):
        for h in range(width // chunk):
            scores = dot(keys[pl.ds(start, tile_cols), :], qt[:, h * chunk : (h + 1) * chunk])
            for l in range(chunk // 128):
                lanes = slice(h * chunk + l * 128, h * chunk + (l + 1) * 128)

                def leaf(g):
                    return jnp.exp2(scores[8 * g : 8 * g + 8, l * 128 : (l + 1) * 128] * scale)

                total, bits = bit_tree(leaf, 0, groups)
                for n, v in enumerate([total, i * total] + bits):
                    acc[n, :, lanes] += v

    def write(shift):
        total, down = acc[0], acc[1]
        along = sum(float(2**b) * acc[2 + b] for b in range(n_bits))
        sub = iota(total.shape, 0).astype(F32)
        first_row = place_ref[0].astype(F32)
        first_col = place_ref[1].astype(F32)
        x = ((2.0 * (first_col + sub) + 1.0) / col_count - 1.0) * total + (16.0 / col_count) * along
        y = ((2.0 * first_row + 1.0) / row_count - 1.0) * total + (2.0 / row_count) * down
        parts = [shift] + [jnp.sum(v, axis=0, keepdims=True) for v in (total, x, y)]
        for p in range(n_block):
            lanes = slice(p * n_query, (p + 1) * n_query)
            block = jnp.concatenate([v[:, lanes] for v in parts], axis=0)
            there = (place_ref[3] + n_block - p) % n_block
            if second:
                out_ref[there, 1 - place_ref[2]] = block
                out_ref[p, place_ref[2]] = other_ref[p]
            else:
                out_ref[there] = block

    sample = jnp.concatenate(
        [keys[i * tile_cols : i * tile_cols + 16, 0:channels] for i in range(0, tile_rows, 2)], axis=0
    )
    shift = jnp.max(dot(sample, qt[0:channels, :]), axis=0, keepdims=True)
    set_shift(shift)
    acc[...] = jnp.zeros_like(acc)
    for i in range(tile_rows):
        add_row(float(i), i * tile_cols)
    write(shift)

    @pl.when(jnp.logical_not(jnp.max(acc[0]) < 1e30))
    def _():
        def raise_max(i, top):
            start = pl.multiple_of(i * tile_cols, tile_cols)
            scores = dot(keys[pl.ds(start, tile_cols), 0:channels], qt[0:channels, :])
            return jnp.maximum(top, jnp.max(scores, axis=0, keepdims=True))

        top = lax.fori_loop(0, tile_rows, raise_max, jnp.full((1, width), -jnp.inf, F32))
        set_shift(top)
        acc[...] = jnp.zeros_like(acc)

        def again(i, carry):
            add_row(i.astype(F32), pl.multiple_of(i * tile_cols, tile_cols))
            return carry

        lax.fori_loop(0, tile_rows, again, 0)
        write(top)


def whole(shape):
    return pl.BlockSpec(shape, lambda *_: (0,) * len(shape))


def merged(states, scale):
    highest = jnp.max(states[:, 0], axis=0)
    factor = jnp.exp2((states[:, 0] - highest[None]) * scale)
    sums = jnp.sum(states[:, 1:] * factor[:, None], axis=0)
    return jnp.concatenate([highest[None], sums], axis=0)


def on_device(frame_two, frame_band, conv_weight):
    channels_in, rows_in, cols_in = frame_two.shape
    channels = conv_weight.shape[1]
    tile_rows, tile_cols = rows_in // 2, cols_in // 2
    band_rows, band_cols = (frame_band.shape[1] - 1) // 2, frame_band.shape[2] // 2
    pb = ("x", "z", "core")
    n_chip, n_pb, n_ka = lax.axis_size(("x", "z")), lax.axis_size(pb), lax.axis_size("ka")
    row_count, col_count = tile_rows * n_pb, tile_cols * n_ka
    pb_index, ka_index = lax.axis_index(pb), lax.axis_index("ka")
    n_query = band_rows * band_cols
    weights = conv_weight.transpose(0, 2, 1)
    params = pltpu.CompilerParams(vmem_limit_bytes=VMEM)

    depth = channels_in * GROUP
    whole_band = (band_rows * 2 + 1, channels_in, 2 * band_cols)
    outs = (
        jax.ShapeDtypeStruct((n_query, channels), BF16),
        jax.ShapeDtypeStruct((2 * band_rows, channels), F32),
        jax.ShapeDtypeStruct((channels_in + 16, cols_in), BF16),
        jax.ShapeDtypeStruct((16, depth), BF16),
    )
    main, edge, down, right = pl.pallas_call(
        query_kernel,
        grid=(1,),
        in_specs=[
            whole(whole_band),
            whole(weights.shape),
            pl.BlockSpec((channels_in, 16, cols_in), lambda i: (0, rows_in // 16 - 1, 0)),
            pl.BlockSpec((channels_in, rows_in, 128), lambda i: (0, 0, cols_in // 128 - 1)),
        ],
        out_specs=[whole(v.shape) for v in outs],
        out_shape=outs,
        compiler_params=params,
        name="query_feats",
    )(frame_band.transpose(1, 0, 2), weights, frame_two, frame_two)
    above = lax.ppermute(down, pb, [(i, i + 1) for i in range(n_pb - 1)])
    place = jnp.stack(
        [
            pb_index * tile_rows,
            ka_index * tile_cols,
            lax.axis_index("core"),
            lax.axis_index("z"),
            lax.axis_index("x"),
        ]
    ).astype(jnp.int32)
    later, edge, place = lax.optimization_barrier((weights, edge, place))
    bands = pl.pallas_call(
        weight_kernel,
        out_shape=jax.ShapeDtypeStruct((3, depth, (GROUP // 2 + 1) * channels), BF16),
        compiler_params=params,
        name="key_weights",
    )(later)
    main, bands, place = lax.optimization_barrier((main, bands, place))
    mine, right = pl.pallas_call(
        join_kernel,
        out_shape=(outs[0], outs[3]),
        compiler_params=params,
        name="query_join",
    )(main, edge, above, right)
    side = lax.ppermute(right, "ka", [(i, i + 1) for i in range(n_ka - 1)])

    def circled(x, axis):
        count = lax.axis_size(axis)
        turns = [[(i, (i + d) % count) for i in range(count)] for d in range(1, count)]
        return jnp.stack([x] + [lax.ppermute(x, axis, pairs) for pairs in turns])

    near, side = lax.optimization_barrier((circled(mine, "z"), side))
    queries = circled(near, "x").reshape(n_chip, n_query, channels)

    n_key = tile_rows * tile_cols
    keys = pl.pallas_call(
        key_kernel,
        out_shape=jax.ShapeDtypeStruct((n_key, channels + 16), BF16),
        compiler_params=params,
        name="key_feats",
    )(frame_two, weights, bands, above, side)
    queries, keys = lax.optimization_barrier((queries, keys))
    twins = lax.ppermute(queries, "core", [(0, 1), (1, 0)])

    n_block, n_x = lax.axis_size("z"), lax.axis_size("x")
    scale = math.log2(math.e) / math.sqrt(channels)

    def attend(block, other):
        def there(i, place):
            return (place[4] + n_x - i) % n_x

        ins = [keys]
        in_specs = [
            pl.BlockSpec((n_block, n_query, channels), lambda i, place: (i, 0, 0)),
            whole(keys.shape),
        ]
        if other is None:
            out_spec = pl.BlockSpec(
                (n_block, 4, n_query), lambda i, place: (there(i, place), 0, 0)
            )
            out_shape = (n_chip, 4, n_query)
        else:
            ins.append(other)
            in_specs.append(
                pl.BlockSpec((n_block, 4, n_query), lambda i, place: (there(i, place), 0, 0))
            )
            out_spec = pl.BlockSpec(
                (n_block, 2, 4, n_query), lambda i, place: (there(i, place), 0, 0, 0)
            )
            out_shape = (n_chip, 2, 4, n_query)
        return pl.pallas_call(
            functools.partial(
                attention_kernel,
                tile_rows, float(row_count), float(col_count), scale, other is not None,
            ),
            grid_spec=pltpu.PrefetchScalarGridSpec(
                num_scalar_prefetch=1,
                grid=(n_x,),
                in_specs=in_specs,
                out_specs=out_spec,
                scratch_shapes=[
                    pltpu.VMEM((channels + 16, n_block * n_query), BF16),
                    pltpu.VMEM((2 + int(math.log2(tile_cols // 8)), 8, n_block * n_query), F32),
                ],
            ),
            out_shape=jax.ShapeDtypeStruct(out_shape, F32),
            compiler_params=params,
            name="attention",
        )(place, block, *ins)

    states = attend(twins, attend(queries, None)).reshape(n_pb, 4, n_query)
    mine = merged(lax.all_to_all(states, pb, 0, 0), scale)
    copies = jnp.broadcast_to(mine[None], (n_ka, 4, n_query))
    final = merged(lax.all_to_all(copies, "ka", 0, 0), scale)
    mean_x = (final[2] / final[1]).reshape(band_rows, band_cols)
    mean_y = (final[3] / final[1]).reshape(band_rows, band_cols)
    query_x = (
        2.0 * (pb_index * band_cols + jnp.arange(band_cols, dtype=jnp.int32)).astype(F32) + 1.0
    ) / col_count - 1.0
    band_top = (row_count - band_rows) // 2
    query_y = (
        2.0 * (band_top + jnp.arange(band_rows, dtype=jnp.int32)).astype(F32) + 1.0
    ) / row_count - 1.0
    return jnp.stack([mean_x - query_x[None, :], mean_y - query_y[:, None]])


def solution(mesh):
    n_pb, n_ka = mesh.shape["pb"], mesh.shape["ka"]
    finer = jax.sharding.Mesh(
        mesh.devices.reshape(n_pb // 8, 4, 2, n_ka), ("x", "z", "core", "ka")
    )
    pb = ("x", "z", "core")
    in_specs = (P(None, pb, "ka"), P(None, None, pb), P())
    out_specs = P(None, None, pb)
    return jax.shard_map(
        on_device, mesh=finer, in_specs=in_specs, out_specs=out_specs, check_vma=False
    )
```
